256 devices in a mesh: plane: 16 (over y, x_lo, core), across: 16 (over z, x_hi).
Axes of the slice: x: 4 (x_hi: 2, x_lo: 2; x = x_hi * 2 + x_lo), y: 4, z: 8, core: 2. Of those that a mesh axis runs over, the one named last changes fastest.
Arguments:
- labels: int32 [256, 1024, 1024], P('across', 'plane'), may hold values 0 or 1
- kappa: float32 [256, 1024, 1024], P('across', 'plane'), may hold values from 0.3 to 3
- inflow: float32 [1024, 1024], P('plane'), may hold values from 0.5 to 2
Outputs:
- level_new: float32 [256, 1024, 1024], P('across', 'plane')
- pressure: float32 [1024, 1024], P('plane', 'across')
The draws below stay inside these ranges and needn't reach their ends.
All inputs are finite; a program needn't handle non-finite values. No bound on the sum of `labels` on one device may be relied on, other than what follows from the above.
Results may differ from the reference program's by a relative error of at most 0.000059.
Values sent between devices are 32-bit elements; how exact they have to be, the bound alone decides.
A program may use at most 64 MiB of HBM per device.

```python
import math
import jax
import jax.numpy as jnp
from jax import lax

NY = 1024
ITERS = 4
NX = 1024
NZ = 256


def set_ends(result, rng, smallest, top_value):
    shape = result.shape
    index_at = [jax.random.randint(jax.random.fold_in(rng, axis), (), 0, shape[axis]) for axis in range(len(shape))]
    result = result.at[tuple(index_at)].set(smallest)
    longest = shape.index(max(shape))
    index_at[longest] = (index_at[longest] + 1) % shape[longest]
    return result.at[tuple(index_at)].set(top_value)


def block_scale(rng, extent, pieces, smallest, top_value):
    def one(axis_at, parts):
        draws = jax.random.uniform(jax.random.fold_in(jax.random.fold_in(rng, 6), axis_at), (parts,), jnp.float32, smallest / len(pieces), top_value / len(pieces))
        return jnp.repeat(jnp.exp(draws), extent[axis_at] // parts).reshape((-1,) + (1,) * (len(extent) - axis_at - 1))

    factor_of = one(*pieces[0])
    for cut in pieces[1:]:
        factor_of = factor_of * one(*cut)
    return factor_of


def setup_inputs(seed: int = 0) -> dict:
    streams_of = jax.random.split(jax.random.key(seed), 4)
    return {
        "labels": set_ends((jax.random.randint(streams_of[0], (NZ, NX, NY), 0, 2) < 1).astype(jnp.int32), jax.random.fold_in(streams_of[0], 1), 0, 1),
        "kappa": jnp.clip(jnp.exp(math.log(3.0) - 2.3025851 * jax.random.uniform(streams_of[1], (NZ, NX, NY), jnp.float32) ** block_scale(streams_of[1], (NZ, NX, NY), ((0, 16), (1, 16)), -0.2, 0.2)), 0.3, 3.0),
        "inflow": jnp.clip(jnp.exp(math.log(2.0) - 1.3862944 * jax.random.uniform(streams_of[2], (NX, NY), jnp.float32) ** block_scale(streams_of[2], (NX, NY), ((0, 16),), -0.2, 0.2)), 0.5, 2.0),
    }


front_width = 0.5
time_step = 0.3
leak_rate = 0.05
cheb_low = 0.05
cheb_high = 2.0

def face_terms(padded_conduct):
    center = padded_conduct[1:-1, 1:-1]
    return (0.5 * (center + padded_conduct[2:, 1:-1]), 0.5 * (center + padded_conduct[:-2, 1:-1]), 0.5 * (center + padded_conduct[1:-1, 2:]), 0.5 * (center + padded_conduct[1:-1, :-2]))

def neighbour_sum(faces, padded_field):
    return faces[0] * padded_field[2:, 1:-1] + faces[1] * padded_field[:-2, 1:-1] + faces[2] * padded_field[1:-1, 2:] + faces[3] * padded_field[1:-1, :-2]

def chebyshev(faces, source, diagonal, padder):
    center = (cheb_high + cheb_low) / 2
    radius = (cheb_high - cheb_low) / 2
    sigma_ratio = center / radius
    rho_prev = 1.0 / sigma_ratio
    pressure = jnp.zeros_like(source)
    residue = source
    direction = source / (center * diagonal)
    for sweep_index in range(ITERS):
        pressure = pressure + direction
        if sweep_index < ITERS - 1:
            image = diagonal * direction - neighbour_sum(faces, padder(direction))
            residue = residue - image
            rho_next = 1.0 / (2 * sigma_ratio - rho_prev)
            direction = rho_next * rho_prev * direction + 2 * rho_next / radius * residue / diagonal
            rho_prev = rho_next
    return pressure

def advance(level, padded_level, kappa, flux_norm):
    grad_z = 0.5 * (padded_level[2:, 1:-1, 1:-1] - padded_level[:-2, 1:-1, 1:-1])
    grad_x = 0.5 * (padded_level[1:-1, 2:, 1:-1] - padded_level[1:-1, :-2, 1:-1])
    grad_y = 0.5 * (padded_level[1:-1, 1:-1, 2:] - padded_level[1:-1, 1:-1, :-2])
    slope = jnp.sqrt(grad_z * grad_z + grad_x * grad_x + grad_y * grad_y + 0.25)
    return level + time_step * kappa * flux_norm[None] * slope

def reference(labels, kappa, inflow):
    level = (1.0 - 2.0 * labels.astype(jnp.float32)) * kappa
    tanh_level = jnp.tanh(level / front_width)
    aperture = lax.optimization_barrier(jnp.sum(0.5 * (1.0 + tanh_level), axis=0)) / NZ
    react = lax.optimization_barrier(jnp.sum(kappa * (1.0 - tanh_level * tanh_level), axis=0)) / (2 * front_width * NZ)
    conduct = aperture ** 3 + 0.05
    rows = jnp.arange(NX).astype(jnp.float32)
    ramp = 1.0 + 2.0 * rows / (NX - 1)
    source = ramp[:, None] * inflow + react
    faces = face_terms(jnp.pad(conduct, 1))
    diagonal = faces[0] + faces[1] + faces[2] + faces[3] + leak_rate
    pressure = chebyshev(faces, source, diagonal, lambda field: jnp.pad(field, 1))
    padded_press = jnp.pad(pressure, 1)
    grad_x = 0.5 * (padded_press[2:, 1:-1] - padded_press[:-2, 1:-1])
    grad_y = 0.5 * (padded_press[1:-1, 2:] - padded_press[1:-1, :-2])
    flux = conduct * (grad_x * grad_x + grad_y * grad_y) + 0.05
    flux_norm = flux / (jnp.sum(flux) / (NX * NY))
    level_new = advance(level, jnp.pad(level, 1), kappa, flux_norm)
    return (level_new, pressure)
```

```python
import functools

import jax
import jax.numpy as jnp
from jax import lax
from jax.experimental import pallas as pl
from jax.experimental.pallas import tpu as pltpu
from jax.sharding import PartitionSpec as P

ITERS = 4

front_width = 0.5
time_step = 0.3
leak_rate = 0.05
cheb_low = 0.05
cheb_high = 2.0

MESH = pl.DeviceIdType.MESH
F32 = jnp.float32

DEPTH = 16
ROWS = 64
WIDTH = 1024
GROUP = 16
LINES = 8
BLOCKS = ROWS // LINES
HALF = WIDTH // 2
STRIP = 128
RING = HALF + STRIP
PAD = 8
CELLS = float(ROWS * GROUP * WIDTH)
VOXELS = float(DEPTH * GROUP)
TOP_ROW = ROWS * GROUP - 1


def far_first(c):
    return 4 + (1 - 2 * lax.rem(c, 2)) * ((c + 1) // 2)


def near_first(c):
    return lax.rem(GROUP + (2 * lax.rem(c, 2) - 1) * ((c + 1) // 2), GROUP)


def aligned(index, step):
    return pl.ds(pl.multiple_of(index * step, step), step)


def kernel(
    labels, kappa, inflow, out, press_out,
    lab, kap, lev, flow, part, got, mine, gathered, rim, rim_got,
    tile, strip, up, down, strip_mid, strip_up, strip_down,
    sums, sums_plane, fluxes, press, press_got,
    lab_sem, kap_sem, flow_sem, xs_sem, xr_sem, zs_sem, zr_sem, hs_sem, hr_sem,
    as_sem, ar_sem, ps_sem, pr_sem, fs_sem, fr_sem, ts_sem, tr_sem, ls_sem, lr_sem, rs_sem, rr_sem,
):
    a = lax.axis_index("across")
    p = lax.axis_index("plane")
    z = a // 2
    xh = lax.rem(a, 2)
    other = 1 - xh
    partner = a + other - xh

    def on_across(index):
        return {"plane": p, "across": index}

    def on_plane(index):
        return {"plane": index, "across": a}

    def ring(index, step):
        return lax.rem(index + step + GROUP, GROUP)

    block_id = p * BLOCKS + z
    count = GROUP * BLOCKS
    before = lax.rem(block_id + count - 1, count)
    after = lax.rem(block_id + 1, count)

    def owner(block, side):
        return {"plane": block // BLOCKS, "across": 2 * lax.rem(block, BLOCKS) + side}

    def send(src, dst, send_sem, recv_sem, device):
        return pltpu.make_async_remote_copy(
            src_ref=src, dst_ref=dst, send_sem=send_sem, recv_sem=recv_sem,
            device_id=device, device_id_type=MESH,
        )

    def block_at(c):
        return lax.rem(z + far_first(c), BLOCKS)

    def load_labels(c):
        rows = aligned(block_at(c), LINES)
        return pltpu.make_async_copy(labels.at[:, rows, :], lab.at[:, rows, :], lab_sem.at[c])

    def load_kappa(c):
        rows = aligned(block_at(c), LINES)
        return pltpu.make_async_copy(kappa.at[:, rows, :], kap.at[:, rows, :], kap_sem.at[c])

    @pl.loop(0, BLOCKS)
    def _(c):
        load_labels(c).start()
        load_kappa(c).start()

    my_rows = aligned(z, LINES)
    my_columns = aligned(xh, HALF)
    load_flow = pltpu.make_async_copy(inflow.at[my_rows, my_columns], flow, flow_sem)
    load_flow.start()

    barrier = pltpu.get_barrier_semaphore()

    @pl.loop(1, GROUP)
    def _(k):
        pl.semaphore_signal(barrier, inc=1, device_id=on_across(ring(a, k)), device_id_type=MESH)
        pl.semaphore_signal(barrier, inc=1, device_id=on_plane(ring(p, k)), device_id_type=MESH)

    for block in (before, after):
        for side in (xh, other):
            pl.semaphore_signal(barrier, inc=1, device_id=owner(block, side), device_id_type=MESH)

    def column_sums(c):
        block = block_at(c)
        rows = aligned(block, LINES)
        load_labels(c).wait()
        load_kappa(c).wait()
        open_sum = jnp.zeros((LINES, WIDTH), F32)
        react_sum = jnp.zeros((LINES, WIDTH), F32)
        for k in range(DEPTH):
            rate = kap[k, rows, :]
            level = jnp.where(lab[k, rows, :] == 0, rate, -rate)
            lev[k + 1, pl.ds(pl.multiple_of(block * LINES + PAD, LINES), LINES), :] = level
            front = jnp.tanh(level * (1.0 / front_width))
            open_sum = open_sum + front
            react_sum = react_sum + rate * (1.0 - front * front)
        for side in range(2):
            part[side, block, 0] = open_sum[:, side * HALF : (side + 1) * HALF]
            part[side, block, 1] = react_sum[:, side * HALF : (side + 1) * HALF]

    def to_partner(c):
        block = block_at(c)
        return send(part.at[other, block], got.at[c], xs_sem.at[c], xr_sem.at[c], on_across(partner))

    early = 4

    @pl.loop(0, early)
    def _(c):
        column_sums(c)

    pl.semaphore_wait(barrier, 2 * (GROUP - 1) + 4)

    @pl.loop(0, early)
    def _(c):
        to_partner(c).start()

    @pl.loop(early, BLOCKS)
    def _(c):
        column_sums(c)
        to_partner(c).start()

    for k in range(DEPTH):
        rim[0, k : k + 1, :] = lev[k + 1, PAD : PAD + 1, :]
        rim[1, k : k + 1, :] = lev[k + 1, PAD + ROWS - 1 : PAD + ROWS, :]
    rims = [
        send(rim.at[0], rim_got.at[1], rs_sem.at[0], rr_sem.at[0], on_plane(ring(p, -1))),
        send(rim.at[1], rim_got.at[0], rs_sem.at[1], rr_sem.at[1], on_plane(ring(p, 1))),
    ]
    for copy in rims:
        copy.start()

    def to_owner(c):
        return send(
            mine.at[c], gathered.at[c], zs_sem.at[c], zr_sem.at[c],
            on_across(2 * block_at(c) + xh),
        )

    @pl.loop(0, BLOCKS - 1)
    def _(c):
        to_partner(c).wait_recv()
        mine[c] = part[xh, block_at(c)] + got[c]
        to_owner(c).start()

    to_partner(BLOCKS - 1).wait_recv()
    mine[BLOCKS - 1] = part[xh, z] + got[BLOCKS - 1]

    body = pl.ds(PAD, ROWS)
    layers = [
        send(lev.at[1, body, :], lev.at[DEPTH + 1, body, :], ls_sem.at[0], lr_sem.at[0], on_across(ring(a, -1))),
        send(lev.at[DEPTH, body, :], lev.at[0, body, :], ls_sem.at[1], lr_sem.at[1], on_across(ring(a, 1))),
    ]
    for copy in layers:
        copy.start()

    for copy in rims:
        copy.wait_recv()
    for k in range(DEPTH):
        lev[k + 1, PAD - 1 : PAD, :] = jnp.where(p == 0, 0.0, rim_got[0, k : k + 1, :])
        lev[k + 1, PAD + ROWS : PAD + ROWS + 1, :] = jnp.where(p == GROUP - 1, 0.0, rim_got[1, k : k + 1, :])

    lane = lax.broadcasted_iota(jnp.int32, (LINES, WIDTH), 1)

    def growth(k):
        for block in range(BLOCKS):
            first = PAD + block * LINES
            here = lev[k + 1, first : first + LINES, :]
            dz = lev[k + 2, first : first + LINES, :] - lev[k, first : first + LINES, :]
            dx = lev[k + 1, first + 1 : first + LINES + 1, :] - lev[k + 1, first - 1 : first + LINES - 1, :]
            right = jnp.where(lane == WIDTH - 1, 0.0, pltpu.roll(here, WIDTH - 1, 1))
            left = jnp.where(lane == 0, 0.0, pltpu.roll(here, 1, 1))
            dy = right - left
            slope = jnp.sqrt(dz * dz + dx * dx + dy * dy + 1.0)
            kap[k, block * LINES : (block + 1) * LINES, :] = (0.5 * time_step) * jnp.abs(here) * slope

    @pl.loop(1, DEPTH - 1)
    def _(k):
        growth(k)

    open_sum = mine[BLOCKS - 1, 0]
    react_sum = mine[BLOCKS - 1, 1]
    for c in range(BLOCKS - 1):
        to_owner(c).wait_recv()
        open_sum = open_sum + gathered[c, 0]
        react_sum = react_sum + gathered[c, 1]
    aperture = 0.5 + open_sum * (0.5 / VOXELS)
    react = react_sum * (1.0 / (2 * front_width * VOXELS))
    load_flow.wait()
    row = (block_id * LINES + lax.broadcasted_iota(jnp.int32, (LINES, HALF), 0)).astype(F32)
    tile[0] = aperture * aperture * aperture + 0.05
    tile[1] = (1.0 + 2.0 * row / TOP_ROW) * flow[...] + react
    strip[...] = tile[:, :, pl.ds(pl.multiple_of(other * (HALF - STRIP), STRIP), STRIP)]

    rims_of_tile = [
        send(tile, down, hs_sem.at[0], hr_sem.at[0], owner(before, xh)),
        send(tile, up, hs_sem.at[1], hr_sem.at[1], owner(after, xh)),
        send(strip, strip_down, hs_sem.at[2], hr_sem.at[2], owner(before, other)),
        send(strip, strip_up, hs_sem.at[3], hr_sem.at[3], owner(after, other)),
        send(strip, strip_mid, hs_sem.at[4], hr_sem.at[4], on_across(partner)),
    ]
    for copy in rims_of_tile:
        copy.start()
    for copy in rims_of_tile:
        copy.wait_recv()

    at_top = block_id == 0
    at_foot = block_id == count - 1

    def around(f):
        above = jnp.concatenate([up[f], strip_up[f]], axis=1)
        level_with = jnp.concatenate([tile[f], strip_mid[f]], axis=1)
        below = jnp.concatenate([down[f], strip_down[f]], axis=1)
        return jnp.concatenate(
            [jnp.where(at_top, 0.0, above), level_with, jnp.where(at_foot, 0.0, below)], axis=0
        )

    shape = (3 * LINES, RING)
    row_at = (block_id - 1) * LINES + lax.broadcasted_iota(jnp.int32, shape, 0)
    column_at = lax.broadcasted_iota(jnp.int32, shape, 1)
    has_up = row_at != 0
    has_down = row_at != TOP_ROW
    has_left = column_at != xh * HALF
    has_right = column_at != RING - 1 - xh * STRIP

    def from_up(v):
        return pltpu.roll(v, 1, 0)

    def from_down(v):
        return pltpu.roll(v, 3 * LINES - 1, 0)

    def from_left(v):
        return pltpu.roll(v, 1, 1)

    def from_right(v):
        return pltpu.roll(v, RING - 1, 1)

    sides = ((from_down, has_down), (from_up, has_up), (from_right, has_right), (from_left, has_left))
    conduct = around(0)
    residue = around(1)
    diagonal = jnp.full(shape, leak_rate, F32)
    weights = []
    for shift, inside in sides:
        face = 0.5 * (conduct + jnp.where(inside, shift(conduct), 0.0))
        diagonal = diagonal + face
        weights.append(jnp.where(inside, face, 0.0))
    inverse = 1.0 / diagonal
    center = (cheb_high + cheb_low) / 2
    radius = (cheb_high - cheb_low) / 2
    sigma_ratio = center / radius
    rho_prev = 1.0 / sigma_ratio
    pressure = jnp.zeros(shape, F32)
    direction = residue * inverse * (1.0 / center)
    for sweep_index in range(ITERS):
        pressure = pressure + direction
        if sweep_index < ITERS - 1:
            image = diagonal * direction
            for weight, (shift, _) in zip(weights, sides):
                image = image - weight * shift(direction)
            residue = residue - image
            rho_next = 1.0 / (2 * sigma_ratio - rho_prev)
            direction = rho_next * rho_prev * direction + (2 * rho_next / radius) * (residue * inverse)
            rho_prev = rho_next
    grad = []
    for shift, inside in sides:
        grad.append(jnp.where(inside, shift(pressure), 0.0))
    grad_x = 0.5 * (grad[0] - grad[1])
    grad_y = 0.5 * (grad[2] - grad[3])
    flux = (conduct * (grad_x * grad_x + grad_y * grad_y) + 0.05)[LINES : 2 * LINES, :HALF]
    fluxes[0] = flux
    total = flux[:, 0:STRIP]
    for c in range(1, HALF // STRIP):
        total = total + flux[:, c * STRIP : (c + 1) * STRIP]
    sums[0] = total
    for c in range(HALF // STRIP):
        press[c] = pressure[LINES : 2 * LINES, c * STRIP : (c + 1) * STRIP]

    def sum_across(k):
        return send(sums.at[0], sums.at[k], as_sem.at[k], ar_sem.at[k], on_across(ring(a, k)))

    def sum_plane(k):
        return send(sums_plane.at[0], sums_plane.at[k], ps_sem.at[k], pr_sem.at[k], on_plane(ring(p, k)))

    def flux_across(k):
        return send(fluxes.at[0], fluxes.at[k], fs_sem.at[k], fr_sem.at[k], on_across(ring(a, k)))

    @pl.loop(0, GROUP - 1)
    def _(c):
        sum_across(near_first(GROUP - 1 - c)).start()

    @pl.loop(0, GROUP - 1)
    def _(c):
        flux_across(near_first(GROUP - 1 - c)).start()

    def to_columns(j):
        return send(press.at[j // 2], press_got.at[z], ts_sem.at[j], tr_sem.at[z], on_across(BLOCKS * xh + j))

    @pl.loop(0, BLOCKS)
    def _(j):
        @pl.when(BLOCKS * xh + j != a)
        def _():
            to_columns(j).start()

        @pl.when(BLOCKS * xh + j == a)
        def _():
            press_got[z] = press[j // 2]

    @pl.loop(1, GROUP)
    def _(k):
        sum_across(k).wait_recv()

    total = sums[0]
    for k in range(1, GROUP):
        total = total + sums[k]
    sums_plane[0] = total

    @pl.loop(1, GROUP)
    def _(k):
        sum_plane(k).start()

    for copy in layers:
        copy.wait_recv()

    @pl.when(a == 0)
    def _():
        lev[0, PAD : PAD + ROWS, :] = jnp.zeros((ROWS, WIDTH), F32)

    @pl.when(a == GROUP - 1)
    def _():
        lev[DEPTH + 1, PAD : PAD + ROWS, :] = jnp.zeros((ROWS, WIDTH), F32)

    growth(0)
    growth(DEPTH - 1)

    @pl.loop(1, GROUP)
    def _(k):
        sum_plane(k).wait_recv()

    total = sums_plane[0]
    for k in range(1, GROUP):
        total = total + sums_plane[k]
    scale = CELLS / jnp.sum(jnp.sum(total, axis=0, keepdims=True), axis=1, keepdims=True)

    def advance(k):
        source = ring(a, -k)
        rows = aligned(source // 2, LINES)
        rows_lev = pl.ds(pl.multiple_of((source // 2) * LINES + PAD, LINES), LINES)
        columns = aligned(lax.rem(source, 2), HALF)
        norm = fluxes[k] * scale
        for layer in range(DEPTH):
            out[layer, rows, columns] = lev[layer + 1, rows_lev, columns] + kap[layer, rows, columns] * norm

    advance(0)

    @pl.loop(1, GROUP)
    def _(c):
        k = near_first(c)
        flux_across(k).wait_recv()
        advance(k)

    @pl.loop(0, BLOCKS)
    def _(source):
        @pl.when(2 * source + a // BLOCKS != a)
        def _():
            send(
                press.at[0], press_got.at[source], ts_sem.at[0], tr_sem.at[source],
                on_across(ring(2 * source + a // BLOCKS, 0)),
            ).wait_recv()

    for block in range(BLOCKS):
        piece = press_got[block]
        piece = jnp.where(xh == 1, pltpu.roll(piece, STRIP // 2, 1), piece)
        press_out[block * LINES : (block + 1) * LINES, :] = piece[:, : STRIP // 2]

    @pl.loop(0, BLOCKS)
    def _(c):
        to_partner(c).wait_send()

    @pl.loop(0, BLOCKS - 1)
    def _(c):
        to_owner(c).wait_send()

    for copy in rims + layers + rims_of_tile:
        copy.wait_send()

    @pl.loop(1, GROUP)
    def _(k):
        sum_across(k).wait_send()
        sum_plane(k).wait_send()
        flux_across(k).wait_send()

    @pl.loop(0, BLOCKS)
    def _(j):
        @pl.when(BLOCKS * xh + j != a)
        def _():
            to_columns(j).wait_send()


def on_device(labels, kappa, inflow):
    vmem = functools.partial(pltpu.VMEM, dtype=F32)
    dma = lambda n: pltpu.SemaphoreType.DMA((n,))
    hbm = pl.BlockSpec(memory_space=pltpu.HBM)
    whole = pl.BlockSpec(memory_space=pltpu.VMEM)
    labels, kappa, inflow = (pltpu.with_memory_space_constraint(x, pltpu.HBM) for x in (labels, kappa, inflow))
    return pl.pallas_call(
        kernel,
        out_shape=(
            jax.ShapeDtypeStruct((DEPTH, ROWS, WIDTH), F32),
            jax.ShapeDtypeStruct((ROWS, STRIP // 2), F32),
        ),
        in_specs=[hbm, hbm, hbm],
        out_specs=(whole, whole),
        scratch_shapes=[
            pltpu.VMEM((DEPTH, ROWS, WIDTH), jnp.int32),
            vmem((DEPTH, ROWS, WIDTH)),
            vmem((DEPTH + 2, ROWS + 2 * PAD, WIDTH)),
            vmem((LINES, HALF)),
            vmem((2, BLOCKS, 2, LINES, HALF)),
            vmem((BLOCKS, 2, LINES, HALF)),
            vmem((BLOCKS, 2, LINES, HALF)),
            vmem((BLOCKS, 2, LINES, HALF)),
            vmem((2, DEPTH, WIDTH)),
            vmem((2, DEPTH, WIDTH)),
            vmem((2, LINES, HALF)),
            vmem((2, LINES, STRIP)),
            vmem((2, LINES, HALF)),
            vmem((2, LINES, HALF)),
            vmem((2, LINES, STRIP)),
            vmem((2, LINES, STRIP)),
            vmem((2, LINES, STRIP)),
            vmem((GROUP, LINES, STRIP)),
            vmem((GROUP, LINES, STRIP)),
            vmem((GROUP, LINES, HALF)),
            vmem((HALF // STRIP, LINES, STRIP)),
            vmem((BLOCKS, LINES, STRIP)),
            dma(BLOCKS), dma(BLOCKS), pltpu.SemaphoreType.DMA,
            dma(BLOCKS), dma(BLOCKS),
            dma(BLOCKS), dma(BLOCKS),
            dma(5), dma(5),
            dma(GROUP), dma(GROUP), dma(GROUP), dma(GROUP),
            dma(GROUP), dma(GROUP),
            dma(BLOCKS), dma(BLOCKS),
            dma(2), dma(2), dma(2), dma(2),
        ],
        compiler_params=pltpu.CompilerParams(
            collective_id=0, has_side_effects=True, vmem_limit_bytes=40 * 2**20
        ),
        cost_estimate=pl.CostEstimate(
            flops=60 * DEPTH * ROWS * WIDTH, bytes_accessed=12 * DEPTH * ROWS * WIDTH,
            transcendentals=2 * DEPTH * ROWS * WIDTH,
        ),
        name="step",
    )(labels, kappa, inflow)


def solution(mesh):
    return jax.shard_map(
        on_device,
        mesh=mesh,
        in_specs=(P("across", "plane", None), P("across", "plane", None), P("plane", None)),
        out_specs=(P("across", "plane", None), P("plane", "across")),
        check_vma=False,
    )
```

```python
import functools

import jax
import jax.numpy as jnp
from jax import lax
from jax.experimental import pallas as pl
from jax.experimental.pallas import tpu as pltpu
from jax.sharding import PartitionSpec as P

ITERS = 4

front_width = 0.5
time_step = 0.3
leak_rate = 0.05
cheb_low = 0.05
cheb_high = 2.0

MESH = pl.DeviceIdType.MESH
F32 = jnp.float32

DEPTH = 16
ROWS = 64
WIDTH = 1024
GROUP = 16
LINES = 8
BLOCKS = ROWS // LINES
LAST = BLOCKS - 1
HALF = WIDTH // 2
STRIP = 128
PAD = 8
CELLS = float(ROWS * GROUP * WIDTH)
VOXELS = float(DEPTH * GROUP)
TOP_ROW = ROWS * GROUP - 1

EARLY = 2
FIRST = 3


def far_first(c):
    return 4 + (1 - 2 * (c % 2)) * ((c + 1) // 2)


def aligned(index, step):
    return pl.ds(pl.multiple_of(index * step, step), step)


def kernel(
    labels, kappa, inflow, lev, kap, fluxes, scale, press_got,
    lab, flow, part, got, mine, gathered, crossed, relay, rim, rim_got, tile, around, sums, sums_plane, press,
    lab_sem, kap_sem, flow_sem, xs_sem, xr_sem, zs_sem, zr_sem, ds_sem, dr_sem, hs_sem, hr_sem,
    as_sem, ar_sem, ps_sem, pr_sem, fs_sem, fr_sem, ts_sem, tr_sem, ls_sem, lr_sem, rs_sem, rr_sem,
):
    a = lax.axis_index("across")
    p = lax.axis_index("plane")
    z = a // 2
    xh = lax.rem(a, 2)
    other = 1 - xh
    partner = a + other - xh

    def on_across(index):
        return {"plane": p, "across": index}

    def on_plane(index):
        return {"plane": index, "across": a}

    def ring(index, step):
        return lax.rem(index + step + GROUP, GROUP)

    block_id = p * BLOCKS + z
    count = GROUP * BLOCKS
    before = lax.rem(block_id + count - 1, count)
    after = lax.rem(block_id + 1, count)

    def owner(block, side):
        return {"plane": block // BLOCKS, "across": 2 * lax.rem(block, BLOCKS) + side}

    def send(src, dst, send_sem, recv_sem, device):
        return pltpu.make_async_remote_copy(
            src_ref=src, dst_ref=dst, send_sem=send_sem, recv_sem=recv_sem,
            device_id=device, device_id_type=MESH,
        )

    def block_at(c):
        return lax.rem(z + far_first(c), BLOCKS)

    def load_labels(c):
        rows = aligned(block_at(c), LINES)
        return pltpu.make_async_copy(labels.at[:, rows, :], lab.at[:, rows, :], lab_sem.at[c])

    def load_kappa(c):
        rows = aligned(block_at(c), LINES)
        return pltpu.make_async_copy(kappa.at[:, rows, :], kap.at[:, rows, :], kap_sem.at[c])

    @pl.loop(0, BLOCKS)
    def _(c):
        load_labels(c).start()
        load_kappa(c).start()

    my_columns = aligned(xh, HALF)
    load_flow = pltpu.make_async_copy(inflow.at[aligned(z, LINES), my_columns], flow, flow_sem)
    load_flow.start()

    barrier = pltpu.get_barrier_semaphore()

    def greet(device):
        pl.semaphore_signal(barrier, inc=1, device_id=device, device_id_type=MESH)

    for k in range(1, BLOCKS):
        greet(on_across(ring(a, 2 * k)))
    for c in range(FIRST, LAST):
        greet(on_across(2 * block_at(c) + other))
    for block in (before, after):
        for side in (xh, other):
            greet(owner(block, side))
    greet(on_across(partner))

    @pl.loop(1, GROUP)
    def _(k):
        greet(on_plane(ring(p, k)))

    greetings = LAST + (LAST - FIRST) + 4 + 1 + GROUP - 1

    def column_sums(c):
        block = block_at(c)
        rows = aligned(block, LINES)
        load_labels(c).wait()
        load_kappa(c).wait()
        open_sum = jnp.zeros((LINES, WIDTH), F32)
        react_sum = jnp.zeros((LINES, WIDTH), F32)
        for k in range(DEPTH):
            rate = kap[k, rows, :]
            level = jnp.where(lab[k, rows, :] == 0, rate, -rate)
            lev[k + 1, pl.ds(pl.multiple_of(block * LINES + PAD, LINES), LINES), :] = level
            front = jnp.tanh(level * (1.0 / front_width))
            open_sum = open_sum + front
            react_sum = react_sum + rate * (1.0 - front * front)
        for side in range(2):
            part[side, block, 0] = open_sum[:, side * HALF : (side + 1) * HALF]
            part[side, block, 1] = react_sum[:, side * HALF : (side + 1) * HALF]

    def to_partner(c):
        block = block_at(c)
        return send(part.at[other, block], got.at[c], xs_sem.at[c], xr_sem.at[c], on_across(partner))

    def to_owner(c, src):
        return send(src, gathered.at[c], zs_sem.at[c], zr_sem.at[c], on_across(2 * block_at(c) + xh))

    def to_other_owner(c):
        block = block_at(c)
        return send(
            part.at[other, block], crossed.at[c], ds_sem.at[c], dr_sem.at[c], on_across(2 * block + other)
        )

    def pass_on(c):
        if isinstance(c, int) and c == LAST:
            to_partner(c).start()
            return

        @pl.when(c < FIRST)
        def _():
            to_partner(c).start()

        @pl.when(c >= FIRST)
        def _():
            to_other_owner(c).start()
            to_owner(c, part.at[xh, block_at(c)]).start()

    @pl.loop(0, EARLY)
    def _(c):
        column_sums(c)

    pl.semaphore_wait(barrier, greetings)

    @pl.loop(0, EARLY)
    def _(c):
        pass_on(c)

    @pl.loop(EARLY, LAST)
    def _(c):
        column_sums(c)
        pass_on(c)

    column_sums(LAST)
    pass_on(LAST)

    body = pl.ds(PAD, ROWS)
    layer_same = send(
        lev.at[1 + other * (DEPTH - 1), body, :], lev.at[xh * (DEPTH + 1), body, :],
        ls_sem.at[0], lr_sem.at[0], on_across(partner),
    )
    layer_hop = send(
        lev.at[1 + xh * (DEPTH - 1), body, :], relay,
        ls_sem.at[1], lr_sem.at[1], on_across(ring(a, 4 * xh - 2)),
    )
    layer_turn = send(
        relay, lev.at[other * (DEPTH + 1), body, :], ls_sem.at[2], lr_sem.at[2], on_across(partner)
    )
    layers = [layer_same, layer_hop, layer_turn]

    for k in range(DEPTH):
        rim[0, k : k + 1, :] = lev[k + 1, PAD : PAD + 1, :]
        rim[1, k : k + 1, :] = lev[k + 1, PAD + ROWS - 1 : PAD + ROWS, :]
    rims = [
        send(rim.at[0], rim_got.at[1], rs_sem.at[0], rr_sem.at[0], on_plane(ring(p, -1))),
        send(rim.at[1], rim_got.at[0], rs_sem.at[1], rr_sem.at[1], on_plane(ring(p, 1))),
    ]
    for copy in rims:
        copy.start()

    @pl.loop(0, FIRST)
    def _(c):
        to_partner(c).wait_recv()
        mine[c] = part[xh, block_at(c)] + got[c]
        to_owner(c, mine.at[c]).start()

    layer_hop.start()

    to_partner(LAST).wait_recv()
    open_sum = part[xh, z, 0] + got[LAST, 0]
    react_sum = part[xh, z, 1] + got[LAST, 1]
    for c in range(LAST):
        to_owner(c, mine.at[c]).wait_recv()
        open_sum = open_sum + gathered[c, 0]
        react_sum = react_sum + gathered[c, 1]
    for c in range(FIRST, LAST):
        to_other_owner(c).wait_recv()
        open_sum = open_sum + crossed[c, 0]
        react_sum = react_sum + crossed[c, 1]
    aperture = 0.5 + open_sum * (0.5 / VOXELS)
    react = react_sum * (1.0 / (2 * front_width * VOXELS))
    load_flow.wait()
    row = (block_id * LINES + lax.broadcasted_iota(jnp.int32, (LINES, HALF), 0)).astype(F32)
    tile[0] = aperture * aperture * aperture + 0.05
    tile[1] = (1.0 + 2.0 * row / TOP_ROW) * flow[...] + react

    def to_around(line, device, k):
        return send(
            tile, around.at[:, pl.ds(line * LINES, LINES), my_columns], hs_sem.at[k], hr_sem.at[k], device
        )

    tiles = [
        to_around(2, owner(before, other), 0),
        to_around(0, owner(after, other), 1),
        to_around(2, owner(before, xh), 2),
        to_around(0, owner(after, xh), 3),
        to_around(1, on_across(partner), 4),
    ]
    for copy in tiles:
        copy.start()
    around[:, LINES : 2 * LINES, my_columns] = tile[...]
    layer_same.start()

    for copy in rims:
        copy.wait_recv()
    for k in range(DEPTH):
        lev[k + 1, PAD - 1 : PAD, :] = jnp.where(p == 0, 0.0, rim_got[0, k : k + 1, :])
        lev[k + 1, PAD + ROWS : PAD + ROWS + 1, :] = jnp.where(p == GROUP - 1, 0.0, rim_got[1, k : k + 1, :])

    lane = lax.broadcasted_iota(jnp.int32, (LINES, WIDTH), 1)

    def growth(k):
        for block in range(BLOCKS):
            first = PAD + block * LINES
            here = lev[k + 1, first : first + LINES, :]
            dz = lev[k + 2, first : first + LINES, :] - lev[k, first : first + LINES, :]
            dx = lev[k + 1, first + 1 : first + LINES + 1, :] - lev[k + 1, first - 1 : first + LINES - 1, :]
            right = jnp.where(lane == WIDTH - 1, 0.0, pltpu.roll(here, WIDTH - 1, 1))
            left = jnp.where(lane == 0, 0.0, pltpu.roll(here, 1, 1))
            dy = right - left
            slope = jnp.sqrt(dz * dz + dx * dx + dy * dy + 1.0)
            kap[k, block * LINES : (block + 1) * LINES, :] = (0.5 * time_step) * jnp.abs(here) * slope

    @pl.loop(1, DEPTH - 1)
    def _(k):
        growth(k)

    for copy in tiles:
        copy.wait_recv()

    shape = (3 * LINES, WIDTH)
    row_at = (block_id - 1) * LINES + lax.broadcasted_iota(jnp.int32, shape, 0)
    column_at = lax.broadcasted_iota(jnp.int32, shape, 1)
    within = jnp.logical_and(row_at >= 0, row_at <= TOP_ROW)
    has_up = row_at != 0
    has_down = row_at != TOP_ROW
    has_left = column_at != 0
    has_right = column_at != WIDTH - 1

    def from_up(v):
        return pltpu.roll(v, 1, 0)

    def from_down(v):
        return pltpu.roll(v, 3 * LINES - 1, 0)

    def from_left(v):
        return pltpu.roll(v, 1, 1)

    def from_right(v):
        return pltpu.roll(v, WIDTH - 1, 1)

    sides = ((from_down, has_down), (from_up, has_up), (from_right, has_right), (from_left, has_left))
    conduct = jnp.where(within, around[0], 0.0)
    residue = jnp.where(within, around[1], 0.0)
    diagonal = jnp.full(shape, leak_rate, F32)
    weights = []
    for shift, inside in sides:
        face = 0.5 * (conduct + jnp.where(inside, shift(conduct), 0.0))
        diagonal = diagonal + face
        weights.append(jnp.where(inside, face, 0.0))
    inverse = 1.0 / diagonal
    center = (cheb_high + cheb_low) / 2
    radius = (cheb_high - cheb_low) / 2
    sigma_ratio = center / radius
    rho_prev = 1.0 / sigma_ratio
    pressure = jnp.zeros(shape, F32)
    direction = residue * inverse * (1.0 / center)
    for sweep_index in range(ITERS):
        pressure = pressure + direction
        if sweep_index < ITERS - 1:
            image = diagonal * direction
            for weight, (shift, _) in zip(weights, sides):
                image = image - weight * shift(direction)
            residue = residue - image
            rho_next = 1.0 / (2 * sigma_ratio - rho_prev)
            direction = rho_next * rho_prev * direction + (2 * rho_next / radius) * (residue * inverse)
            rho_prev = rho_next
    grad = []
    for shift, inside in sides:
        grad.append(jnp.where(inside, shift(pressure), 0.0))
    grad_x = 0.5 * (grad[0] - grad[1])
    grad_y = 0.5 * (grad[2] - grad[3])
    flux = (conduct * (grad_x * grad_x + grad_y * grad_y) + 0.05)[LINES : 2 * LINES]
    total = flux[:, 0:STRIP]
    for c in range(1, WIDTH // STRIP):
        total = total + flux[:, c * STRIP : (c + 1) * STRIP]
    sums[0] = total

    def sum_blocks(k):
        return send(sums.at[0], sums.at[k], as_sem.at[k], ar_sem.at[k], on_across(ring(a, 2 * k)))

    def sum_plane(k):
        return send(sums_plane.at[0], sums_plane.at[k], ps_sem.at[k], pr_sem.at[k], on_plane(ring(p, k)))

    def flux_out(k):
        return send(fluxes.at[z], fluxes.at[z], fs_sem.at[k], fr_sem.at[k], on_across(ring(a, 2 * k)))

    def press_out(k):
        return send(
            press.at[lax.rem(z + k, BLOCKS)], press_got.at[z], ts_sem.at[k], tr_sem.at[k],
            on_across(ring(a, 2 * k)),
        )

    @pl.loop(0, LAST)
    def _(c):
        sum_blocks(far_first(c)).start()

    fluxes[z] = flux

    @pl.loop(0, LAST)
    def _(c):
        flux_out(far_first(c)).start()

    layer_hop.wait_recv()
    layer_turn.start()

    for c in range(BLOCKS):
        press[c] = pressure[LINES : 2 * LINES, c * STRIP : (c + 1) * STRIP]
    press_got[z] = press[z]

    @pl.loop(1, BLOCKS)
    def _(k):
        sum_blocks(k).wait_recv()

    total = sums[0]
    for k in range(1, BLOCKS):
        total = total + sums[k]
    sums_plane[0] = total

    @pl.loop(1, GROUP)
    def _(k):
        sum_plane(k).start()

    @pl.loop(1, BLOCKS)
    def _(k):
        press_out(k).start()

    layer_same.wait_recv()
    layer_turn.wait_recv()

    @pl.when(a == GROUP - 1)
    def _():
        lev[DEPTH + 1, PAD : PAD + ROWS, :] = jnp.zeros((ROWS, WIDTH), F32)

    growth(DEPTH - 1)

    @pl.when(a == 0)
    def _():
        lev[0, PAD : PAD + ROWS, :] = jnp.zeros((ROWS, WIDTH), F32)

    growth(0)

    @pl.loop(1, GROUP)
    def _(k):
        sum_plane(k).wait_recv()

    total = sums_plane[0]
    for k in range(1, GROUP):
        total = total + sums_plane[k]
    total = jnp.sum(jnp.sum(total, axis=0, keepdims=True), axis=1, keepdims=True)
    scale[...] = jnp.broadcast_to(CELLS / total, scale.shape)

    @pl.loop(1, BLOCKS)
    def _(k):
        flux_out(k).wait_recv()
        press_out(k).wait_recv()

    @pl.loop(0, FIRST)
    def _(c):
        to_partner(c).wait_send()

    to_partner(LAST).wait_send()

    @pl.loop(0, LAST)
    def _(c):
        to_owner(c, mine.at[c]).wait_send()

    @pl.loop(FIRST, LAST)
    def _(c):
        to_other_owner(c).wait_send()

    for copy in [*rims, *layers, *tiles]:
        copy.wait_send()

    @pl.loop(1, BLOCKS)
    def _(k):
        sum_blocks(k).wait_send()
        flux_out(k).wait_send()
        press_out(k).wait_send()

    @pl.loop(1, GROUP)
    def _(k):
        sum_plane(k).wait_send()


def finish(lev, kap, fluxes, scale, press_got, level_new, pressure, level_at, press_at, level_sem, press_sem):
    xh = lax.rem(lax.axis_index("across"), 2)

    def store(block):
        rows = aligned(block, LINES)
        return pltpu.make_async_copy(level_at.at[:, rows, :], level_new.at[:, rows, :], level_sem.at[block])

    @pl.loop(0, BLOCKS)
    def _(block):
        rows = aligned(block, LINES)
        rows_lev = pl.ds(pl.multiple_of(block * LINES + PAD, LINES), LINES)
        norm = fluxes[block] * scale[0:1, 0:1]
        for k in range(DEPTH):
            level_at[k, rows, :] = lev[k + 1, rows_lev, :] + kap[k, rows, :] * norm
        store(block).start()

    for block in range(BLOCKS):
        piece = press_got[block]
        piece = jnp.where(xh == 1, pltpu.roll(piece, STRIP // 2, 1), piece)
        press_at[block * LINES : (block + 1) * LINES, :] = piece[:, : STRIP // 2]
    store_press = pltpu.make_async_copy(press_at, pressure, press_sem)
    store_press.start()

    @pl.loop(0, BLOCKS)
    def _(block):
        store(block).wait()

    store_press.wait()


def on_device(labels, kappa, inflow):
    vmem = functools.partial(pltpu.VMEM, dtype=F32)
    dma = lambda n: pltpu.SemaphoreType.DMA((n,))
    hbm = pl.BlockSpec(memory_space=pltpu.HBM)
    whole = pl.BlockSpec(memory_space=pltpu.VMEM)
    labels, kappa, inflow = (pltpu.with_memory_space_constraint(x, pltpu.HBM) for x in (labels, kappa, inflow))
    parts = pl.pallas_call(
        kernel,
        out_shape=(
            jax.ShapeDtypeStruct((DEPTH + 2, ROWS + 2 * PAD, WIDTH), F32),
            jax.ShapeDtypeStruct((DEPTH, ROWS, WIDTH), F32),
            jax.ShapeDtypeStruct((BLOCKS, LINES, WIDTH), F32),
            jax.ShapeDtypeStruct((LINES, STRIP), F32),
            jax.ShapeDtypeStruct((BLOCKS, LINES, STRIP), F32),
        ),
        in_specs=[hbm, hbm, hbm],
        out_specs=(whole,) * 5,
        scratch_shapes=[
            pltpu.VMEM((DEPTH, ROWS, WIDTH), jnp.int32),
            vmem((LINES, HALF)),
            vmem((2, BLOCKS, 2, LINES, HALF)),
            vmem((BLOCKS, 2, LINES, HALF)),
            vmem((LAST, 2, LINES, HALF)),
            vmem((LAST, 2, LINES, HALF)),
            vmem((LAST, 2, LINES, HALF)),
            vmem((ROWS, WIDTH)),
            vmem((2, DEPTH, WIDTH)),
            vmem((2, DEPTH, WIDTH)),
            vmem((2, LINES, HALF)),
            vmem((2, 3 * LINES, WIDTH)),
            vmem((BLOCKS, LINES, STRIP)),
            vmem((GROUP, LINES, STRIP)),
            vmem((BLOCKS, LINES, STRIP)),
            dma(BLOCKS), dma(BLOCKS), pltpu.SemaphoreType.DMA,
            dma(BLOCKS), dma(BLOCKS),
            dma(BLOCKS), dma(BLOCKS), dma(BLOCKS), dma(BLOCKS),
            dma(5), dma(5),
            dma(BLOCKS), dma(BLOCKS), dma(GROUP), dma(GROUP),
            dma(BLOCKS), dma(BLOCKS), dma(BLOCKS), dma(BLOCKS),
            dma(3), dma(3), dma(2), dma(2),
        ],
        compiler_params=pltpu.CompilerParams(
            collective_id=0, has_side_effects=True, vmem_limit_bytes=32 * 2**20
        ),
        cost_estimate=pl.CostEstimate(
            flops=60 * DEPTH * ROWS * WIDTH, bytes_accessed=8 * DEPTH * ROWS * WIDTH,
            transcendentals=2 * DEPTH * ROWS * WIDTH,
        ),
        name="step",
    )(labels, kappa, inflow)
    return pl.pallas_call(
        finish,
        out_shape=(
            jax.ShapeDtypeStruct((DEPTH, ROWS, WIDTH), F32),
            jax.ShapeDtypeStruct((ROWS, STRIP // 2), F32),
        ),
        in_specs=[whole] * 5,
        out_specs=(hbm, hbm),
        scratch_shapes=[
            vmem((DEPTH, ROWS, WIDTH)),
            vmem((ROWS, STRIP // 2)),
            dma(BLOCKS),
            pltpu.SemaphoreType.DMA,
        ],
        compiler_params=pltpu.CompilerParams(vmem_limit_bytes=16 * 2**20),
        cost_estimate=pl.CostEstimate(
            flops=2 * DEPTH * ROWS * WIDTH, bytes_accessed=4 * DEPTH * ROWS * WIDTH, transcendentals=0
        ),
        name="finish",
    )(*parts)


def solution(mesh):
    return jax.shard_map(
        on_device,
        mesh=mesh,
        in_specs=(P("across", "plane", None), P("across", "plane", None), P("plane", None)),
        out_specs=(P("across", "plane", None), P("plane", "across")),
        check_vma=False,
    )
```

```python
import functools

import jax
import jax.numpy as jnp
from jax import lax
from jax.experimental import pallas as pl
from jax.experimental.pallas import tpu as pltpu
from jax.sharding import PartitionSpec as P

ITERS = 4

front_width = 0.5
time_step = 0.3
leak_rate = 0.05
cheb_low = 0.05
cheb_high = 2.0

MESH = pl.DeviceIdType.MESH
F32 = jnp.float32

DEPTH = 16
ROWS = 64
WIDTH = 1024
GROUP = 16
LINES = 8
BLOCKS = ROWS // LINES
LAST = BLOCKS - 1
HALF = WIDTH // 2
STRIP = 128
PAD = 8
CELLS = float(ROWS * GROUP * WIDTH)
VOXELS = float(DEPTH * GROUP)
TOP_ROW = ROWS * GROUP - 1

EARLY = (8, 8, 8, 4, 1, 1, 1, 1)
ORDER = (4, 2, 3, 6, 5, 1, 7, 0)
VIA = (0, 2, 4)
STRAIGHT = (1, 3, 5, 6)


def pick(table, c):
    if isinstance(c, int):
        return table[c]
    value = table[0]
    for index in range(1, len(table)):
        value = jnp.where(c == index, table[index], value)
    return value


def far_first(c):
    return 4 + (1 - 2 * (c % 2)) * ((c + 1) // 2)


def aligned(index, step):
    return pl.ds(pl.multiple_of(index * step, step), step)


def kernel(
    labels, kappa, inflow, lev, kap, fluxes, scale, press_got,
    lab, flow, part, got, mine, gathered, crossed, relay, rim, rim_got, tile, around, sums, sums_plane, press,
    lab_sem, kap_sem, flow_sem, xs_sem, xr_sem, zs_sem, zr_sem, ds_sem, dr_sem, hs_sem, hr_sem,
    as_sem, ar_sem, ps_sem, pr_sem, fs_sem, fr_sem, ts_sem, tr_sem, ls_sem, lr_sem, rs_sem, rr_sem,
):
    a = lax.axis_index("across")
    p = lax.axis_index("plane")
    z = a // 2
    xh = lax.rem(a, 2)
    other = 1 - xh
    partner = a + other - xh

    def on_across(index):
        return {"plane": p, "across": index}

    def on_plane(index):
        return {"plane": index, "across": a}

    def ring(index, step):
        return lax.rem(index + step + GROUP, GROUP)

    block_id = p * BLOCKS + z
    count = GROUP * BLOCKS
    before = lax.rem(block_id + count - 1, count)
    after = lax.rem(block_id + 1, count)

    def owner(block, side):
        return {"plane": block // BLOCKS, "across": 2 * lax.rem(block, BLOCKS) + side}

    def send(src, dst, send_sem, recv_sem, device):
        return pltpu.make_async_remote_copy(
            src_ref=src, dst_ref=dst, send_sem=send_sem, recv_sem=recv_sem,
            device_id=device, device_id_type=MESH,
        )

    def block_at(c):
        return lax.rem(z + pick(ORDER, c), BLOCKS)

    def load_labels(c):
        rows = aligned(block_at(c), LINES)
        return pltpu.make_async_copy(labels.at[:, rows, :], lab.at[:, rows, :], lab_sem.at[c])

    def load_kappa(c):
        rows = aligned(block_at(c), LINES)
        return pltpu.make_async_copy(kappa.at[:, rows, :], kap.at[:, rows, :], kap_sem.at[c])

    @pl.loop(0, BLOCKS)
    def _(c):
        load_labels(c).start()
        load_kappa(c).start()

    my_columns = aligned(xh, HALF)
    load_flow = pltpu.make_async_copy(inflow.at[aligned(z, LINES), my_columns], flow, flow_sem)
    load_flow.start()

    barrier = pltpu.get_barrier_semaphore()

    def greet(device):
        pl.semaphore_signal(barrier, inc=1, device_id=device, device_id_type=MESH)

    for k in range(1, BLOCKS):
        greet(on_across(ring(a, 2 * k)))
    for c in STRAIGHT:
        greet(on_across(2 * block_at(c) + other))
    for block in (before, after):
        for side in (xh, other):
            greet(owner(block, side))
    greet(on_across(partner))

    @pl.loop(1, GROUP)
    def _(k):
        greet(on_plane(ring(p, k)))

    greetings = LAST + len(STRAIGHT) + 4 + 1 + GROUP - 1

    def column_sums(c):
        block = block_at(c)
        rows = aligned(block, LINES)
        load_labels(c).wait()
        load_kappa(c).wait()
        open_sum = jnp.zeros((LINES, WIDTH), F32)
        react_sum = jnp.zeros((LINES, WIDTH), F32)
        for k in range(DEPTH):
            rate = kap[k, rows, :]
            level = jnp.where(lab[k, rows, :] == 0, rate, -rate)
            lev[k + 1, pl.ds(pl.multiple_of(block * LINES + PAD, LINES), LINES), :] = level
            front = jnp.tanh(level * (1.0 / front_width))
            open_sum = open_sum + front
            react_sum = react_sum + rate * (1.0 - front * front)
        for side in range(2):
            part[side, block, 0] = open_sum[:, side * HALF : (side + 1) * HALF]
            part[side, block, 1] = react_sum[:, side * HALF : (side + 1) * HALF]

    def to_partner(c):
        block = block_at(c)
        return send(part.at[other, block], got.at[c], xs_sem.at[c], xr_sem.at[c], on_across(partner))

    def to_owner(c, src):
        return send(src, gathered.at[c], zs_sem.at[c], zr_sem.at[c], on_across(2 * block_at(c) + xh))

    def to_other_owner(c):
        block = block_at(c)
        return send(
            part.at[other, block], crossed.at[c], ds_sem.at[c], dr_sem.at[c], on_across(2 * block + other)
        )

    def pass_on(c):
        via = pick(tuple(int(k in VIA or k == LAST) for k in range(BLOCKS)), c) == 1

        @pl.when(via)
        def _():
            to_partner(c).start()

        @pl.when(jnp.logical_not(via))
        def _():
            to_owner(c, part.at[xh, block_at(c)]).start()
            to_other_owner(c).start()

    early = pick(EARLY, z)

    @pl.loop(0, early)
    def _(c):
        column_sums(c)

    pl.semaphore_wait(barrier, greetings)

    @pl.loop(0, early)
    def _(c):
        pass_on(c)

    @pl.loop(early, BLOCKS)
    def _(c):
        column_sums(c)
        pass_on(c)

    body = pl.ds(PAD, ROWS)
    layer_same = send(
        lev.at[1 + other * (DEPTH - 1), body, :], lev.at[xh * (DEPTH + 1), body, :],
        ls_sem.at[0], lr_sem.at[0], on_across(partner),
    )
    layer_hop = send(
        lev.at[1 + xh * (DEPTH - 1), body, :], relay,
        ls_sem.at[1], lr_sem.at[1], on_across(ring(a, 4 * xh - 2)),
    )
    layer_turn = send(
        relay, lev.at[other * (DEPTH + 1), body, :], ls_sem.at[2], lr_sem.at[2], on_across(partner)
    )
    layers = [layer_same, layer_hop, layer_turn]

    for k in range(DEPTH):
        rim[0, k : k + 1, :] = lev[k + 1, PAD : PAD + 1, :]
        rim[1, k : k + 1, :] = lev[k + 1, PAD + ROWS - 1 : PAD + ROWS, :]
    rims = [
        send(rim.at[0], rim_got.at[1], rs_sem.at[0], rr_sem.at[0], on_plane(ring(p, -1))),
        send(rim.at[1], rim_got.at[0], rs_sem.at[1], rr_sem.at[1], on_plane(ring(p, 1))),
    ]
    for copy in rims:
        copy.start()

    @pl.loop(0, len(VIA))
    def _(k):
        c = pick(VIA, k)
        to_partner(c).wait_recv()
        mine[c] = part[xh, block_at(c)] + got[c]
        to_owner(c, mine.at[c]).start()

    layer_hop.start()

    to_partner(LAST).wait_recv()
    open_sum = part[xh, z, 0] + got[LAST, 0]
    react_sum = part[xh, z, 1] + got[LAST, 1]
    for c in range(LAST):
        to_owner(c, mine.at[c]).wait_recv()
        open_sum = open_sum + gathered[c, 0]
        react_sum = react_sum + gathered[c, 1]
    for c in STRAIGHT:
        to_other_owner(c).wait_recv()
        open_sum = open_sum + crossed[c, 0]
        react_sum = react_sum + crossed[c, 1]
    aperture = 0.5 + open_sum * (0.5 / VOXELS)
    react = react_sum * (1.0 / (2 * front_width * VOXELS))
    load_flow.wait()
    row = (block_id * LINES + lax.broadcasted_iota(jnp.int32, (LINES, HALF), 0)).astype(F32)
    tile[0] = aperture * aperture * aperture + 0.05
    tile[1] = (1.0 + 2.0 * row / TOP_ROW) * flow[...] + react

    def to_around(line, device, k):
        return send(
            tile, around.at[:, pl.ds(line * LINES, LINES), my_columns], hs_sem.at[k], hr_sem.at[k], device
        )

    tiles = [
        to_around(2, owner(before, other), 0),
        to_around(0, owner(after, other), 1),
        to_around(2, owner(before, xh), 2),
        to_around(0, owner(after, xh), 3),
        to_around(1, on_across(partner), 4),
    ]
    for copy in tiles:
        copy.start()
    around[:, LINES : 2 * LINES, my_columns] = tile[...]
    layer_same.start()

    for copy in rims:
        copy.wait_recv()
    for k in range(DEPTH):
        lev[k + 1, PAD - 1 : PAD, :] = jnp.where(p == 0, 0.0, rim_got[0, k : k + 1, :])
        lev[k + 1, PAD + ROWS : PAD + ROWS + 1, :] = jnp.where(p == GROUP - 1, 0.0, rim_got[1, k : k + 1, :])

    lane = lax.broadcasted_iota(jnp.int32, (LINES, WIDTH), 1)

    def growth(k):
        for block in range(BLOCKS):
            first = PAD + block * LINES
            here = lev[k + 1, first : first + LINES, :]
            dz = lev[k + 2, first : first + LINES, :] - lev[k, first : first + LINES, :]
            dx = lev[k + 1, first + 1 : first + LINES + 1, :] - lev[k + 1, first - 1 : first + LINES - 1, :]
            right = jnp.where(lane == WIDTH - 1, 0.0, pltpu.roll(here, WIDTH - 1, 1))
            left = jnp.where(lane == 0, 0.0, pltpu.roll(here, 1, 1))
            dy = right - left
            slope = jnp.sqrt(dz * dz + dx * dx + dy * dy + 1.0)
            kap[k, block * LINES : (block + 1) * LINES, :] = (0.5 * time_step) * jnp.abs(here) * slope

    @pl.loop(1, DEPTH - 1)
    def _(k):
        growth(k)

    for copy in tiles:
        copy.wait_recv()

    shape = (3 * LINES, WIDTH)
    row_at = (block_id - 1) * LINES + lax.broadcasted_iota(jnp.int32, shape, 0)
    column_at = lax.broadcasted_iota(jnp.int32, shape, 1)
    within = jnp.logical_and(row_at >= 0, row_at <= TOP_ROW)
    has_up = row_at != 0
    has_down = row_at != TOP_ROW
    has_left = column_at != 0
    has_right = column_at != WIDTH - 1

    def from_up(v):
        return pltpu.roll(v, 1, 0)

    def from_down(v):
        return pltpu.roll(v, 3 * LINES - 1, 0)

    def from_left(v):
        return pltpu.roll(v, 1, 1)

    def from_right(v):
        return pltpu.roll(v, WIDTH - 1, 1)

    sides = ((from_down, has_down), (from_up, has_up), (from_right, has_right), (from_left, has_left))
    conduct = jnp.where(within, around[0], 0.0)
    residue = jnp.where(within, around[1], 0.0)
    diagonal = jnp.full(shape, leak_rate, F32)
    weights = []
    for shift, inside in sides:
        face = 0.5 * (conduct + jnp.where(inside, shift(conduct), 0.0))
        diagonal = diagonal + face
        weights.append(jnp.where(inside, face, 0.0))
    inverse = 1.0 / diagonal
    center = (cheb_high + cheb_low) / 2
    radius = (cheb_high - cheb_low) / 2
    sigma_ratio = center / radius
    rho_prev = 1.0 / sigma_ratio
    pressure = jnp.zeros(shape, F32)
    direction = residue * inverse * (1.0 / center)
    for sweep_index in range(ITERS):
        pressure = pressure + direction
        if sweep_index < ITERS - 1:
            image = diagonal * direction
            for weight, (shift, _) in zip(weights, sides):
                image = image - weight * shift(direction)
            residue = residue - image
            rho_next = 1.0 / (2 * sigma_ratio - rho_prev)
            direction = rho_next * rho_prev * direction + (2 * rho_next / radius) * (residue * inverse)
            rho_prev = rho_next
    grad = []
    for shift, inside in sides:
        grad.append(jnp.where(inside, shift(pressure), 0.0))
    grad_x = 0.5 * (grad[0] - grad[1])
    grad_y = 0.5 * (grad[2] - grad[3])
    flux = (conduct * (grad_x * grad_x + grad_y * grad_y) + 0.05)[LINES : 2 * LINES]
    total = flux[:, 0:STRIP]
    for c in range(1, WIDTH // STRIP):
        total = total + flux[:, c * STRIP : (c + 1) * STRIP]
    sums[0] = jnp.sum(total, axis=0, keepdims=True)

    def sum_blocks(k):
        return send(sums.at[0], sums.at[k], as_sem.at[k], ar_sem.at[k], on_across(ring(a, 2 * k)))

    def sum_plane(k):
        return send(sums_plane.at[0], sums_plane.at[k], ps_sem.at[k], pr_sem.at[k], on_plane(ring(p, k)))

    def flux_out(k):
        return send(fluxes.at[z], fluxes.at[z], fs_sem.at[k], fr_sem.at[k], on_across(ring(a, 2 * k)))

    def press_out(k):
        return send(
            press.at[lax.rem(z + k, BLOCKS)], press_got.at[z], ts_sem.at[k], tr_sem.at[k],
            on_across(ring(a, 2 * k)),
        )

    @pl.loop(0, LAST)
    def _(c):
        sum_blocks(far_first(c)).start()

    fluxes[z] = flux

    @pl.loop(0, BLOCKS)
    def _(reached):
        @pl.when(reached != z)
        def _():
            flux_out(lax.rem(reached - z + BLOCKS, BLOCKS)).start()

    layer_hop.wait_recv()
    layer_turn.start()

    for c in range(BLOCKS):
        press[c] = pressure[LINES : 2 * LINES, c * STRIP : (c + 1) * STRIP]
    press_got[z] = press[z]

    @pl.loop(1, BLOCKS)
    def _(k):
        sum_blocks(k).wait_recv()

    total = sums[0]
    for k in range(1, BLOCKS):
        total = total + sums[k]
    sums_plane[0] = total

    @pl.loop(1, GROUP)
    def _(k):
        sum_plane(k).start()

    @pl.loop(1, BLOCKS)
    def _(k):
        press_out(k).start()

    layer_same.wait_recv()
    layer_turn.wait_recv()

    @pl.when(a == GROUP - 1)
    def _():
        lev[DEPTH + 1, PAD : PAD + ROWS, :] = jnp.zeros((ROWS, WIDTH), F32)

    growth(DEPTH - 1)

    @pl.when(a == 0)
    def _():
        lev[0, PAD : PAD + ROWS, :] = jnp.zeros((ROWS, WIDTH), F32)

    growth(0)

    @pl.loop(1, GROUP)
    def _(k):
        sum_plane(k).wait_recv()

    total = sums_plane[0]
    for k in range(1, GROUP):
        total = total + sums_plane[k]
    total = jnp.sum(total, axis=1, keepdims=True)
    scale[...] = jnp.broadcast_to(CELLS / total, scale.shape)

    @pl.loop(1, BLOCKS)
    def _(k):
        flux_out(k).wait_recv()
        press_out(k).wait_recv()

    @pl.loop(0, len(VIA))
    def _(k):
        to_partner(pick(VIA, k)).wait_send()

    to_partner(LAST).wait_send()

    @pl.loop(0, LAST)
    def _(c):
        to_owner(c, mine.at[c]).wait_send()

    for c in STRAIGHT:
        to_other_owner(c).wait_send()

    for copy in [*rims, *layers, *tiles]:
        copy.wait_send()

    @pl.loop(1, BLOCKS)
    def _(k):
        sum_blocks(k).wait_send()
        flux_out(k).wait_send()
        press_out(k).wait_send()

    @pl.loop(1, GROUP)
    def _(k):
        sum_plane(k).wait_send()


def finish(lev, kap, fluxes, scale, press_got, level_new, pressure, level_at, press_at, level_sem, press_sem):
    xh = lax.rem(lax.axis_index("across"), 2)

    def store(block):
        rows = aligned(block, LINES)
        return pltpu.make_async_copy(level_at.at[:, rows, :], level_new.at[:, rows, :], level_sem.at[block])

    @pl.loop(0, BLOCKS)
    def _(block):
        rows = aligned(block, LINES)
        rows_lev = pl.ds(pl.multiple_of(block * LINES + PAD, LINES), LINES)
        norm = fluxes[block] * scale[0:1, 0:1]
        for k in range(DEPTH):
            level_at[k, rows, :] = lev[k + 1, rows_lev, :] + kap[k, rows, :] * norm
        store(block).start()

    for block in range(BLOCKS):
        piece = press_got[block]
        piece = jnp.where(xh == 1, pltpu.roll(piece, STRIP // 2, 1), piece)
        press_at[block * LINES : (block + 1) * LINES, :] = piece[:, : STRIP // 2]
    store_press = pltpu.make_async_copy(press_at, pressure, press_sem)
    store_press.start()

    @pl.loop(0, BLOCKS)
    def _(block):
        store(block).wait()

    store_press.wait()


def on_device(labels, kappa, inflow):
    vmem = functools.partial(pltpu.VMEM, dtype=F32)
    dma = lambda n: pltpu.SemaphoreType.DMA((n,))
    hbm = pl.BlockSpec(memory_space=pltpu.HBM)
    whole = pl.BlockSpec(memory_space=pltpu.VMEM)
    labels, kappa, inflow = (pltpu.with_memory_space_constraint(x, pltpu.HBM) for x in (labels, kappa, inflow))
    parts = pl.pallas_call(
        kernel,
        out_shape=(
            jax.ShapeDtypeStruct((DEPTH + 2, ROWS + 2 * PAD, WIDTH), F32),
            jax.ShapeDtypeStruct((DEPTH, ROWS, WIDTH), F32),
            jax.ShapeDtypeStruct((BLOCKS, LINES, WIDTH), F32),
            jax.ShapeDtypeStruct((LINES, STRIP), F32),
            jax.ShapeDtypeStruct((BLOCKS, LINES, STRIP), F32),
        ),
        in_specs=[hbm, hbm, hbm],
        out_specs=(whole,) * 5,
        scratch_shapes=[
            pltpu.VMEM((DEPTH, ROWS, WIDTH), jnp.int32),
            vmem((LINES, HALF)),
            vmem((2, BLOCKS, 2, LINES, HALF)),
            vmem((BLOCKS, 2, LINES, HALF)),
            vmem((LAST, 2, LINES, HALF)),
            vmem((LAST, 2, LINES, HALF)),
            vmem((LAST, 2, LINES, HALF)),
            vmem((ROWS, WIDTH)),
            vmem((2, DEPTH, WIDTH)),
            vmem((2, DEPTH, WIDTH)),
            vmem((2, LINES, HALF)),
            vmem((2, 3 * LINES, WIDTH)),
            vmem((BLOCKS, 1, STRIP)),
            vmem((GROUP, 1, STRIP)),
            vmem((BLOCKS, LINES, STRIP)),
            dma(BLOCKS), dma(BLOCKS), pltpu.SemaphoreType.DMA,
            dma(BLOCKS), dma(BLOCKS),
            dma(BLOCKS), dma(BLOCKS), dma(BLOCKS), dma(BLOCKS),
            dma(5), dma(5),
            dma(BLOCKS), dma(BLOCKS), dma(GROUP), dma(GROUP),
            dma(BLOCKS), dma(BLOCKS), dma(BLOCKS), dma(BLOCKS),
            dma(3), dma(3), dma(2), dma(2),
        ],
        compiler_params=pltpu.CompilerParams(
            collective_id=0, has_side_effects=True, vmem_limit_bytes=32 * 2**20
        ),
        cost_estimate=pl.CostEstimate(
            flops=60 * DEPTH * ROWS * WIDTH, bytes_accessed=8 * DEPTH * ROWS * WIDTH,
            transcendentals=2 * DEPTH * ROWS * WIDTH,
        ),
        name="step",
    )(labels, kappa, inflow)
    return pl.pallas_call(
        finish,
        out_shape=(
            jax.ShapeDtypeStruct((DEPTH, ROWS, WIDTH), F32),
            jax.ShapeDtypeStruct((ROWS, STRIP // 2), F32),
        ),
        in_specs=[whole] * 5,
        out_specs=(hbm, hbm),
        scratch_shapes=[
            vmem((DEPTH, ROWS, WIDTH)),
            vmem((ROWS, STRIP // 2)),
            dma(BLOCKS),
            pltpu.SemaphoreType.DMA,
        ],
        compiler_params=pltpu.CompilerParams(vmem_limit_bytes=16 * 2**20),
        cost_estimate=pl.CostEstimate(
            flops=2 * DEPTH * ROWS * WIDTH, bytes_accessed=4 * DEPTH * ROWS * WIDTH, transcendentals=0
        ),
        name="finish",
    )(*parts)


def solution(mesh):
    return jax.shard_map(
        on_device,
        mesh=mesh,
        in_specs=(P("across", "plane", None), P("across", "plane", None), P("plane", None)),
        out_specs=(P("across", "plane", None), P("plane", "across")),
        check_vma=False,
    )
```

```python
import functools

import jax
import jax.numpy as jnp
from jax import lax
from jax.experimental import pallas as pl
from jax.experimental.pallas import tpu as pltpu
from jax.sharding import PartitionSpec as P

ITERS = 4

front_width = 0.5
time_step = 0.3
leak_rate = 0.05
cheb_low = 0.05
cheb_high = 2.0

MESH = pl.DeviceIdType.MESH
F32 = jnp.float32

DEPTH = 16
ROWS = 64
WIDTH = 1024
GROUP = 16
LINES = 8
BLOCKS = ROWS // LINES
LAST = BLOCKS - 1
HALF = WIDTH // 2
STRIP = 128
PAD = 8
CELLS = float(ROWS * GROUP * WIDTH)
VOXELS = float(DEPTH * GROUP)
TOP_ROW = ROWS * GROUP - 1

EARLY = (8, 8, 8, 4, 1, 1, 1, 1)
ORDER = (4, 2, 3, 6, 5, 1, 7, 0)
VIA = (0, 2, 4)
STRAIGHT = (1, 3, 5, 6)


def pick(table, c):
    if isinstance(c, int):
        return table[c]
    value = table[0]
    for index in range(1, len(table)):
        value = jnp.where(c == index, table[index], value)
    return value


def far_first(c):
    return 4 + (1 - 2 * (c % 2)) * ((c + 1) // 2)


def aligned(index, step):
    return pl.ds(pl.multiple_of(index * step, step), step)


def kernel(
    labels, kappa, inflow, lev, kap, fluxes, scale, press_got,
    lab, flow, part, got, mine, gathered, crossed, relay, rim, rim_got, tile, around, sums, sums_plane, press,
    lab_sem, kap_sem, flow_sem, xs_sem, xr_sem, zs_sem, zr_sem, ds_sem, dr_sem, hs_sem, hr_sem,
    as_sem, ar_sem, ps_sem, pr_sem, fs_sem, fr_sem, ts_sem, tr_sem, ls_sem, lr_sem, rs_sem, rr_sem,
):
    a = lax.axis_index("across")
    p = lax.axis_index("plane")
    z = a // 2
    xh = lax.rem(a, 2)
    other = 1 - xh
    partner = a + other - xh

    def on_across(index):
        return {"plane": p, "across": index}

    def on_plane(index):
        return {"plane": index, "across": a}

    def ring(index, step):
        return lax.rem(index + step + GROUP, GROUP)

    block_id = p * BLOCKS + z
    count = GROUP * BLOCKS
    before = lax.rem(block_id + count - 1, count)
    after = lax.rem(block_id + 1, count)

    def owner(block, side):
        return {"plane": block // BLOCKS, "across": 2 * lax.rem(block, BLOCKS) + side}

    def send(src, dst, send_sem, recv_sem, device):
        return pltpu.make_async_remote_copy(
            src_ref=src, dst_ref=dst, send_sem=send_sem, recv_sem=recv_sem,
            device_id=device, device_id_type=MESH,
        )

    def block_at(c):
        return lax.rem(z + pick(ORDER, c), BLOCKS)

    def load_labels(c):
        rows = aligned(block_at(c), LINES)
        return pltpu.make_async_copy(labels.at[:, rows, :], lab.at[:, rows, :], lab_sem.at[c])

    def load_kappa(c):
        rows = aligned(block_at(c), LINES)
        return pltpu.make_async_copy(kappa.at[:, rows, :], kap.at[:, rows, :], kap_sem.at[c])

    @pl.loop(0, 2)
    def _(c):
        load_labels(c).start()
        load_kappa(c).start()

    my_columns = aligned(xh, HALF)
    load_flow = pltpu.make_async_copy(inflow.at[aligned(z, LINES), my_columns], flow, flow_sem)
    barrier = pltpu.get_barrier_semaphore()

    def greet(device):
        pl.semaphore_signal(barrier, inc=1, device_id=device, device_id_type=MESH)

    for k in (4, 3, 5, 2, 6, 1, 7):
        greet(on_across(ring(a, 2 * k)))
    for c in STRAIGHT:
        greet(on_across(2 * block_at(c) + other))
    for block in (before, after):
        for side in (xh, other):
            greet(owner(block, side))
    greet(on_across(partner))

    @pl.loop(1, GROUP)
    def _(k):
        greet(on_plane(ring(p, k)))

    @pl.loop(2, BLOCKS)
    def _(c):
        load_labels(c).start()
        load_kappa(c).start()

    load_flow.start()

    greetings = LAST + len(STRAIGHT) + 4 + 1 + GROUP - 1

    def column_sums(c):
        block = block_at(c)
        rows = aligned(block, LINES)
        load_labels(c).wait()
        load_kappa(c).wait()
        open_sum = jnp.zeros((LINES, WIDTH), F32)
        react_sum = jnp.zeros((LINES, WIDTH), F32)
        for k in range(DEPTH):
            rate = kap[k, rows, :]
            level = jnp.where(lab[k, rows, :] == 0, rate, -rate)
            lev[k + 1, pl.ds(pl.multiple_of(block * LINES + PAD, LINES), LINES), :] = level
            front = jnp.tanh(level * (1.0 / front_width))
            open_sum = open_sum + front
            react_sum = react_sum + rate * (1.0 - front * front)
        for side in range(2):
            part[side, block, 0] = open_sum[:, side * HALF : (side + 1) * HALF]
            part[side, block, 1] = react_sum[:, side * HALF : (side + 1) * HALF]

    def to_partner(c):
        block = block_at(c)
        return send(part.at[other, block], got.at[c], xs_sem.at[c], xr_sem.at[c], on_across(partner))

    def to_owner(c, src):
        return send(src, gathered.at[c], zs_sem.at[c], zr_sem.at[c], on_across(2 * block_at(c) + xh))

    def to_other_owner(c):
        block = block_at(c)
        return send(
            part.at[other, block], crossed.at[c], ds_sem.at[c], dr_sem.at[c], on_across(2 * block + other)
        )

    def pass_on(c):
        via = pick(tuple(int(k in VIA or k == LAST) for k in range(BLOCKS)), c) == 1

        @pl.when(via)
        def _():
            to_partner(c).start()

        @pl.when(jnp.logical_not(via))
        def _():
            to_owner(c, part.at[xh, block_at(c)]).start()
            to_other_owner(c).start()

    early = pick(EARLY, z)

    @pl.loop(0, early)
    def _(c):
        column_sums(c)

    pl.semaphore_wait(barrier, greetings)

    @pl.loop(0, early)
    def _(c):
        pass_on(c)

    @pl.loop(early, BLOCKS)
    def _(c):
        column_sums(c)
        pass_on(c)

    body = pl.ds(PAD, ROWS)
    layer_same = send(
        lev.at[1 + other * (DEPTH - 1), body, :], lev.at[xh * (DEPTH + 1), body, :],
        ls_sem.at[0], lr_sem.at[0], on_across(partner),
    )
    layer_hop = send(
        lev.at[1 + xh * (DEPTH - 1), body, :], relay,
        ls_sem.at[1], lr_sem.at[1], on_across(ring(a, 4 * xh - 2)),
    )
    layer_turn = send(
        relay, lev.at[other * (DEPTH + 1), body, :], ls_sem.at[2], lr_sem.at[2], on_across(partner)
    )
    layers = [layer_same, layer_hop, layer_turn]

    for k in range(DEPTH):
        rim[0, k : k + 1, :] = lev[k + 1, PAD : PAD + 1, :]
        rim[1, k : k + 1, :] = lev[k + 1, PAD + ROWS - 1 : PAD + ROWS, :]
    rims = [
        send(rim.at[0], rim_got.at[1], rs_sem.at[0], rr_sem.at[0], on_plane(ring(p, -1))),
        send(rim.at[1], rim_got.at[0], rs_sem.at[1], rr_sem.at[1], on_plane(ring(p, 1))),
    ]
    for copy in rims:
        copy.start()

    @pl.loop(0, len(VIA))
    def _(k):
        c = pick(VIA, k)
        to_partner(c).wait_recv()
        mine[c] = part[xh, block_at(c)] + got[c]
        to_owner(c, mine.at[c]).start()

    layer_hop.start()

    to_partner(LAST).wait_recv()
    open_sum = part[xh, z, 0] + got[LAST, 0]
    react_sum = part[xh, z, 1] + got[LAST, 1]
    for c in range(LAST):
        to_owner(c, mine.at[c]).wait_recv()
        open_sum = open_sum + gathered[c, 0]
        react_sum = react_sum + gathered[c, 1]
    for c in STRAIGHT:
        to_other_owner(c).wait_recv()
        open_sum = open_sum + crossed[c, 0]
        react_sum = react_sum + crossed[c, 1]
    aperture = 0.5 + open_sum * (0.5 / VOXELS)
    react = react_sum * (1.0 / (2 * front_width * VOXELS))
    load_flow.wait()
    row = (block_id * LINES + lax.broadcasted_iota(jnp.int32, (LINES, HALF), 0)).astype(F32)
    tile[0] = aperture * aperture * aperture + 0.05
    tile[1] = (1.0 + 2.0 * row / TOP_ROW) * flow[...] + react

    def to_around(line, device, k):
        return send(
            tile, around.at[:, pl.ds(line * LINES, LINES), my_columns], hs_sem.at[k], hr_sem.at[k], device
        )

    tiles = [
        to_around(2, owner(before, other), 0),
        to_around(0, owner(after, other), 1),
        to_around(2, owner(before, xh), 2),
        to_around(0, owner(after, xh), 3),
        to_around(1, on_across(partner), 4),
    ]
    for copy in tiles:
        copy.start()
    around[:, LINES : 2 * LINES, my_columns] = tile[...]
    layer_same.start()

    for copy in rims:
        copy.wait_recv()
    for k in range(DEPTH):
        lev[k + 1, PAD - 1 : PAD, :] = jnp.where(p == 0, 0.0, rim_got[0, k : k + 1, :])
        lev[k + 1, PAD + ROWS : PAD + ROWS + 1, :] = jnp.where(p == GROUP - 1, 0.0, rim_got[1, k : k + 1, :])

    lane = lax.broadcasted_iota(jnp.int32, (LINES, WIDTH), 1)

    def growth(k):
        for block in range(BLOCKS):
            first = PAD + block * LINES
            here = lev[k + 1, first : first + LINES, :]
            dz = lev[k + 2, first : first + LINES, :] - lev[k, first : first + LINES, :]
            dx = lev[k + 1, first + 1 : first + LINES + 1, :] - lev[k + 1, first - 1 : first + LINES - 1, :]
            right = jnp.where(lane == WIDTH - 1, 0.0, pltpu.roll(here, WIDTH - 1, 1))
            left = jnp.where(lane == 0, 0.0, pltpu.roll(here, 1, 1))
            dy = right - left
            slope = jnp.sqrt(dz * dz + dx * dx + dy * dy + 1.0)
            kap[k, block * LINES : (block + 1) * LINES, :] = (0.5 * time_step) * jnp.abs(here) * slope

    @pl.loop(1, DEPTH - 1)
    def _(k):
        growth(k)

    for copy in tiles:
        copy.wait_recv()

    shape = (3 * LINES, WIDTH)
    row_at = (block_id - 1) * LINES + lax.broadcasted_iota(jnp.int32, shape, 0)
    column_at = lax.broadcasted_iota(jnp.int32, shape, 1)
    within = jnp.logical_and(row_at >= 0, row_at <= TOP_ROW)
    has_up = row_at != 0
    has_down = row_at != TOP_ROW
    has_left = column_at != 0
    has_right = column_at != WIDTH - 1

    def from_up(v):
        return pltpu.roll(v, 1, 0)

    def from_down(v):
        return pltpu.roll(v, 3 * LINES - 1, 0)

    def from_left(v):
        return pltpu.roll(v, 1, 1)

    def from_right(v):
        return pltpu.roll(v, WIDTH - 1, 1)

    sides = ((from_down, has_down), (from_up, has_up), (from_right, has_right), (from_left, has_left))
    conduct = jnp.where(within, around[0], 0.0)
    residue = jnp.where(within, around[1], 0.0)
    diagonal = jnp.full(shape, leak_rate, F32)
    weights = []
    for shift, inside in sides:
        face = 0.5 * (conduct + jnp.where(inside, shift(conduct), 0.0))
        diagonal = diagonal + face
        weights.append(jnp.where(inside, face, 0.0))
    inverse = 1.0 / diagonal
    center = (cheb_high + cheb_low) / 2
    radius = (cheb_high - cheb_low) / 2
    sigma_ratio = center / radius
    rho_prev = 1.0 / sigma_ratio
    pressure = jnp.zeros(shape, F32)
    direction = residue * inverse * (1.0 / center)
    for sweep_index in range(ITERS):
        pressure = pressure + direction
        if sweep_index < ITERS - 1:
            image = diagonal * direction
            for weight, (shift, _) in zip(weights, sides):
                image = image - weight * shift(direction)
            residue = residue - image
            rho_next = 1.0 / (2 * sigma_ratio - rho_prev)
            direction = rho_next * rho_prev * direction + (2 * rho_next / radius) * (residue * inverse)
            rho_prev = rho_next
    grad = []
    for shift, inside in sides:
        grad.append(jnp.where(inside, shift(pressure), 0.0))
    grad_x = 0.5 * (grad[0] - grad[1])
    grad_y = 0.5 * (grad[2] - grad[3])
    flux = (conduct * (grad_x * grad_x + grad_y * grad_y) + 0.05)[LINES : 2 * LINES]
    total = flux[:, 0:STRIP]
    for c in range(1, WIDTH // STRIP):
        total = total + flux[:, c * STRIP : (c + 1) * STRIP]
    sums[0] = jnp.sum(total, axis=0, keepdims=True)

    def sum_blocks(k):
        return send(sums.at[0], sums.at[k], as_sem.at[k], ar_sem.at[k], on_across(ring(a, 2 * k)))

    def sum_plane(k):
        return send(sums_plane.at[0], sums_plane.at[k], ps_sem.at[k], pr_sem.at[k], on_plane(ring(p, k)))

    def flux_out(k):
        return send(fluxes.at[z], fluxes.at[z], fs_sem.at[k], fr_sem.at[k], on_across(ring(a, 2 * k)))

    def press_out(k):
        return send(
            press.at[lax.rem(z + k, BLOCKS)], press_got.at[z], ts_sem.at[k], tr_sem.at[k],
            on_across(ring(a, 2 * k)),
        )

    @pl.loop(0, LAST)
    def _(c):
        sum_blocks(far_first(c)).start()

    fluxes[z] = flux

    @pl.loop(0, BLOCKS)
    def _(reached):
        @pl.when(reached != z)
        def _():
            flux_out(lax.rem(reached - z + BLOCKS, BLOCKS)).start()

    layer_hop.wait_recv()
    layer_turn.start()

    for c in range(BLOCKS):
        press[c] = pressure[LINES : 2 * LINES, c * STRIP : (c + 1) * STRIP]
    press_got[z] = press[z]

    @pl.loop(1, BLOCKS)
    def _(k):
        sum_blocks(k).wait_recv()

    total = sums[0]
    for k in range(1, BLOCKS):
        total = total + sums[k]
    sums_plane[0] = total

    @pl.loop(1, GROUP)
    def _(k):
        sum_plane(k).start()

    @pl.loop(1, BLOCKS)
    def _(k):
        press_out(k).start()

    layer_same.wait_recv()
    layer_turn.wait_recv()

    @pl.when(a == GROUP - 1)
    def _():
        lev[DEPTH + 1, PAD : PAD + ROWS, :] = jnp.zeros((ROWS, WIDTH), F32)

    growth(DEPTH - 1)

    @pl.when(a == 0)
    def _():
        lev[0, PAD : PAD + ROWS, :] = jnp.zeros((ROWS, WIDTH), F32)

    growth(0)

    @pl.loop(0, len(VIA))
    def _(k):
        to_partner(pick(VIA, k)).wait_send()

    to_partner(LAST).wait_send()

    @pl.loop(0, LAST)
    def _(c):
        to_owner(c, mine.at[c]).wait_send()

    for c in STRAIGHT:
        to_other_owner(c).wait_send()

    for copy in [*rims, *layers, *tiles]:
        copy.wait_send()

    @pl.loop(1, BLOCKS)
    def _(k):
        sum_blocks(k).wait_send()
        flux_out(k).wait_send()
        press_out(k).wait_send()

    @pl.loop(1, GROUP)
    def _(k):
        sum_plane(k).wait_send()

    @pl.loop(1, GROUP)
    def _(k):
        sum_plane(k).wait_recv()

    total = sums_plane[0]
    for k in range(1, GROUP):
        total = total + sums_plane[k]
    total = jnp.sum(total, axis=1, keepdims=True)
    scale[...] = jnp.broadcast_to(CELLS / total, scale.shape)

    @pl.loop(1, BLOCKS)
    def _(k):
        flux_out(k).wait_recv()
        press_out(k).wait_recv()


def finish(lev, kap, fluxes, scale, press_got, level_new, pressure, level_at, press_at, level_sem, press_sem):
    xh = lax.rem(lax.axis_index("across"), 2)

    def store(block):
        rows = aligned(block, LINES)
        return pltpu.make_async_copy(level_at.at[:, rows, :], level_new.at[:, rows, :], level_sem.at[block])

    @pl.loop(0, BLOCKS)
    def _(block):
        rows = aligned(block, LINES)
        rows_lev = pl.ds(pl.multiple_of(block * LINES + PAD, LINES), LINES)
        norm = fluxes[block] * scale[0:1, 0:1]
        for k in range(DEPTH):
            level_at[k, rows, :] = lev[k + 1, rows_lev, :] + kap[k, rows, :] * norm
        store(block).start()

    for block in range(BLOCKS):
        piece = press_got[block]
        piece = jnp.where(xh == 1, pltpu.roll(piece, STRIP // 2, 1), piece)
        press_at[block * LINES : (block + 1) * LINES, :] = piece[:, : STRIP // 2]
    store_press = pltpu.make_async_copy(press_at, pressure, press_sem)
    store_press.start()

    @pl.loop(0, BLOCKS)
    def _(block):
        store(block).wait()

    store_press.wait()


def on_device(labels, kappa, inflow):
    vmem = functools.partial(pltpu.VMEM, dtype=F32)
    dma = lambda n: pltpu.SemaphoreType.DMA((n,))
    hbm = pl.BlockSpec(memory_space=pltpu.HBM)
    whole = pl.BlockSpec(memory_space=pltpu.VMEM)
    labels, kappa, inflow = (pltpu.with_memory_space_constraint(x, pltpu.HBM) for x in (labels, kappa, inflow))
    parts = pl.pallas_call(
        kernel,
        out_shape=(
            jax.ShapeDtypeStruct((DEPTH + 2, ROWS + 2 * PAD, WIDTH), F32),
            jax.ShapeDtypeStruct((DEPTH, ROWS, WIDTH), F32),
            jax.ShapeDtypeStruct((BLOCKS, LINES, WIDTH), F32),
            jax.ShapeDtypeStruct((LINES, STRIP), F32),
            jax.ShapeDtypeStruct((BLOCKS, LINES, STRIP), F32),
        ),
        in_specs=[hbm, hbm, hbm],
        out_specs=(whole,) * 5,
        scratch_shapes=[
            pltpu.VMEM((DEPTH, ROWS, WIDTH), jnp.int32),
            vmem((LINES, HALF)),
            vmem((2, BLOCKS, 2, LINES, HALF)),
            vmem((BLOCKS, 2, LINES, HALF)),
            vmem((LAST, 2, LINES, HALF)),
            vmem((LAST, 2, LINES, HALF)),
            vmem((LAST, 2, LINES, HALF)),
            vmem((ROWS, WIDTH)),
            vmem((2, DEPTH, WIDTH)),
            vmem((2, DEPTH, WIDTH)),
            vmem((2, LINES, HALF)),
            vmem((2, 3 * LINES, WIDTH)),
            vmem((BLOCKS, 1, STRIP)),
            vmem((GROUP, 1, STRIP)),
            vmem((BLOCKS, LINES, STRIP)),
            dma(BLOCKS), dma(BLOCKS), pltpu.SemaphoreType.DMA,
            dma(BLOCKS), dma(BLOCKS),
            dma(BLOCKS), dma(BLOCKS), dma(BLOCKS), dma(BLOCKS),
            dma(5), dma(5),
            dma(BLOCKS), dma(BLOCKS), dma(GROUP), dma(GROUP),
            dma(BLOCKS), dma(BLOCKS), dma(BLOCKS), dma(BLOCKS),
            dma(3), dma(3), dma(2), dma(2),
        ],
        compiler_params=pltpu.CompilerParams(
            collective_id=0, has_side_effects=True, vmem_limit_bytes=32 * 2**20
        ),
        cost_estimate=pl.CostEstimate(
            flops=60 * DEPTH * ROWS * WIDTH, bytes_accessed=8 * DEPTH * ROWS * WIDTH,
            transcendentals=2 * DEPTH * ROWS * WIDTH,
        ),
        name="step",
    )(labels, kappa, inflow)
    return pl.pallas_call(
        finish,
        out_shape=(
            jax.ShapeDtypeStruct((DEPTH, ROWS, WIDTH), F32),
            jax.ShapeDtypeStruct((ROWS, STRIP // 2), F32),
        ),
        in_specs=[whole] * 5,
        out_specs=(hbm, hbm),
        scratch_shapes=[
            vmem((DEPTH, ROWS, WIDTH)),
            vmem((ROWS, STRIP // 2)),
            dma(BLOCKS),
            pltpu.SemaphoreType.DMA,
        ],
        compiler_params=pltpu.CompilerParams(vmem_limit_bytes=16 * 2**20),
        cost_estimate=pl.CostEstimate(
            flops=2 * DEPTH * ROWS * WIDTH, bytes_accessed=4 * DEPTH * ROWS * WIDTH, transcendentals=0
        ),
        name="finish",
    )(*parts)


def solution(mesh):
    return jax.shard_map(
        on_device,
        mesh=mesh,
        in_specs=(P("across", "plane", None), P("across", "plane", None), P("plane", None)),
        out_specs=(P("across", "plane", None), P("plane", "across")),
        check_vma=False,
    )
```

```python
import functools

import jax
import jax.numpy as jnp
from jax import lax
from jax.experimental import pallas as pl
from jax.experimental.pallas import tpu as pltpu
from jax.sharding import PartitionSpec as P

ITERS = 4

front_width = 0.5
time_step = 0.3
leak_rate = 0.05
cheb_low = 0.05
cheb_high = 2.0

MESH = pl.DeviceIdType.MESH
F32 = jnp.float32

DEPTH = 16
ROWS = 64
WIDTH = 1024
GROUP = 16
LINES = 8
BLOCKS = ROWS // LINES
LAST = BLOCKS - 1
HALF = WIDTH // 2
STRIP = 128
PAD = 8
CELLS = float(ROWS * GROUP * WIDTH)
VOXELS = float(DEPTH * GROUP)
TOP_ROW = ROWS * GROUP - 1

EARLY = (8, 8, 8, 4, 1, 1, 1, 1)
ORDER = (4, 2, 3, 6, 5, 1, 7, 0)
VIA = (0, 2, 4)
STRAIGHT = (1, 3, 5, 6)


def pick(table, c):
    if isinstance(c, int):
        return table[c]
    value = table[0]
    for index in range(1, len(table)):
        value = jnp.where(c == index, table[index], value)
    return value


def far_first(c):
    return 4 + (1 - 2 * (c % 2)) * ((c + 1) // 2)


def aligned(index, step):
    return pl.ds(pl.multiple_of(index * step, step), step)


def kernel(
    labels, kappa, inflow, lev, kap, fluxes, scale, press_got,
    lab, flow, part, got, mine, gathered, crossed, relay, rim, rim_got, tile, around, sums, sums_plane, press,
    lab_sem, kap_sem, flow_sem, xs_sem, xr_sem, zs_sem, zr_sem, ds_sem, dr_sem, hs_sem, hr_sem,
    as_sem, ar_sem, ps_sem, pr_sem, fs_sem, fr_sem, ts_sem, tr_sem, ls_sem, lr_sem, rs_sem, rr_sem,
):
    a = lax.axis_index("across")
    p = lax.axis_index("plane")
    z = a // 2
    xh = lax.rem(a, 2)
    other = 1 - xh
    partner = a + other - xh

    def on_across(index):
        return {"plane": p, "across": index}

    def on_plane(index):
        return {"plane": index, "across": a}

    def ring(index, step):
        return lax.rem(index + step + GROUP, GROUP)

    block_id = p * BLOCKS + z
    count = GROUP * BLOCKS
    before = lax.rem(block_id + count - 1, count)
    after = lax.rem(block_id + 1, count)

    def owner(block, side):
        return {"plane": block // BLOCKS, "across": 2 * lax.rem(block, BLOCKS) + side}

    def send(src, dst, send_sem, recv_sem, device):
        return pltpu.make_async_remote_copy(
            src_ref=src, dst_ref=dst, send_sem=send_sem, recv_sem=recv_sem,
            device_id=device, device_id_type=MESH,
        )

    def block_at(c):
        return lax.rem(z + pick(ORDER, c), BLOCKS)

    def load_labels(c):
        rows = aligned(block_at(c), LINES)
        return pltpu.make_async_copy(labels.at[:, rows, :], lab.at[:, rows, :], lab_sem.at[c])

    def load_kappa(c):
        rows = aligned(block_at(c), LINES)
        return pltpu.make_async_copy(kappa.at[:, rows, :], kap.at[:, rows, :], kap_sem.at[c])

    @pl.loop(0, BLOCKS)
    def _(c):
        load_labels(c).start()
        load_kappa(c).start()

    my_columns = aligned(xh, HALF)
    load_flow = pltpu.make_async_copy(inflow.at[aligned(z, LINES), my_columns], flow, flow_sem)
    load_flow.start()

    barrier = pltpu.get_barrier_semaphore()

    def greet(device):
        pl.semaphore_signal(barrier, inc=1, device_id=device, device_id_type=MESH)

    for k in range(1, BLOCKS):
        greet(on_across(ring(a, 2 * k)))
    for c in STRAIGHT:
        greet(on_across(2 * block_at(c) + other))
    for block in (before, after):
        for side in (xh, other):
            greet(owner(block, side))
    greet(on_across(partner))

    @pl.loop(1, GROUP)
    def _(k):
        greet(on_plane(ring(p, k)))

    greetings = LAST + len(STRAIGHT) + 4 + 1 + GROUP - 1

    def column_sums(c):
        block = block_at(c)
        rows = aligned(block, LINES)
        load_labels(c).wait()
        load_kappa(c).wait()
        open_sum = jnp.zeros((LINES, WIDTH), F32)
        react_sum = jnp.zeros((LINES, WIDTH), F32)
        for k in range(DEPTH):
            rate = kap[k, rows, :]
            level = jnp.where(lab[k, rows, :] == 0, rate, -rate)
            lev[k + 1, pl.ds(pl.multiple_of(block * LINES + PAD, LINES), LINES), :] = level
            front = jnp.tanh(level * (1.0 / front_width))
            open_sum = open_sum + front
            react_sum = react_sum + rate * (1.0 - front * front)
        for side in range(2):
            part[side, block, 0] = open_sum[:, side * HALF : (side + 1) * HALF]
            part[side, block, 1] = react_sum[:, side * HALF : (side + 1) * HALF]

    def to_partner(c):
        block = block_at(c)
        return send(part.at[other, block], got.at[c], xs_sem.at[c], xr_sem.at[c], on_across(partner))

    def to_owner(c, src):
        return send(src, gathered.at[c], zs_sem.at[c], zr_sem.at[c], on_across(2 * block_at(c) + xh))

    def to_other_owner(c):
        block = block_at(c)
        return send(
            part.at[other, block], crossed.at[c], ds_sem.at[c], dr_sem.at[c], on_across(2 * block + other)
        )

    def pass_on(c):
        via = pick(tuple(int(k in VIA or k == LAST) for k in range(BLOCKS)), c) == 1

        @pl.when(via)
        def _():
            to_partner(c).start()

        @pl.when(jnp.logical_not(via))
        def _():
            to_owner(c, part.at[xh, block_at(c)]).start()
            to_other_owner(c).start()

    early = pick(EARLY, z)

    @pl.loop(0, early)
    def _(c):
        column_sums(c)

    pl.semaphore_wait(barrier, greetings)

    @pl.loop(0, early)
    def _(c):
        pass_on(c)

    @pl.loop(early, BLOCKS)
    def _(c):
        column_sums(c)
        pass_on(c)

    body = pl.ds(PAD, ROWS)
    layer_same = send(
        lev.at[1 + other * (DEPTH - 1), body, :], lev.at[xh * (DEPTH + 1), body, :],
        ls_sem.at[0], lr_sem.at[0], on_across(partner),
    )
    layer_hop = send(
        lev.at[1 + xh * (DEPTH - 1), body, :], relay,
        ls_sem.at[1], lr_sem.at[1], on_across(ring(a, 4 * xh - 2)),
    )
    layer_turn = send(
        relay, lev.at[other * (DEPTH + 1), body, :], ls_sem.at[2], lr_sem.at[2], on_across(partner)
    )
    has_both = jnp.logical_and(a != 0, a != GROUP - 1)
    partner_has_both = jnp.logical_and(partner != 0, partner != GROUP - 1)

    for k in range(DEPTH):
        rim[0, k : k + 1, :] = lev[k + 1, PAD : PAD + 1, :]
        rim[1, k : k + 1, :] = lev[k + 1, PAD + ROWS - 1 : PAD + ROWS, :]
    rims = [
        send(rim.at[0], rim_got.at[1], rs_sem.at[0], rr_sem.at[0], on_plane(ring(p, -1))),
        send(rim.at[1], rim_got.at[0], rs_sem.at[1], rr_sem.at[1], on_plane(ring(p, 1))),
    ]
    for copy in rims:
        copy.start()

    @pl.loop(0, len(VIA))
    def _(k):
        c = pick(VIA, k)
        to_partner(c).wait_recv()
        mine[c] = part[xh, block_at(c)] + got[c]
        to_owner(c, mine.at[c]).start()

    layer_same.start()

    @pl.when(has_both)
    def _():
        layer_hop.start()


    to_partner(LAST).wait_recv()
    open_sum = part[xh, z, 0] + got[LAST, 0]
    react_sum = part[xh, z, 1] + got[LAST, 1]
    for c in range(LAST):
        to_owner(c, mine.at[c]).wait_recv()
        open_sum = open_sum + gathered[c, 0]
        react_sum = react_sum + gathered[c, 1]
    for c in STRAIGHT:
        to_other_owner(c).wait_recv()
        open_sum = open_sum + crossed[c, 0]
        react_sum = react_sum + crossed[c, 1]
    aperture = 0.5 + open_sum * (0.5 / VOXELS)
    react = react_sum * (1.0 / (2 * front_width * VOXELS))
    load_flow.wait()
    row = (block_id * LINES + lax.broadcasted_iota(jnp.int32, (LINES, HALF), 0)).astype(F32)
    tile[0] = aperture * aperture * aperture + 0.05
    tile[1] = (1.0 + 2.0 * row / TOP_ROW) * flow[...] + react

    def to_around(line, device, k):
        return send(
            tile, around.at[:, pl.ds(line * LINES, LINES), my_columns], hs_sem.at[k], hr_sem.at[k], device
        )

    tiles = [
        to_around(2, owner(before, other), 0),
        to_around(0, owner(after, other), 1),
        to_around(2, owner(before, xh), 2),
        to_around(0, owner(after, xh), 3),
        to_around(1, on_across(partner), 4),
    ]
    for copy in tiles:
        copy.start()
    around[:, LINES : 2 * LINES, my_columns] = tile[...]

    for copy in rims:
        copy.wait_recv()
    for k in range(DEPTH):
        lev[k + 1, PAD - 1 : PAD, :] = jnp.where(p == 0, 0.0, rim_got[0, k : k + 1, :])
        lev[k + 1, PAD + ROWS : PAD + ROWS + 1, :] = jnp.where(p == GROUP - 1, 0.0, rim_got[1, k : k + 1, :])

    lane = lax.broadcasted_iota(jnp.int32, (LINES, WIDTH), 1)

    def growth(k):
        for block in range(BLOCKS):
            first = PAD + block * LINES
            here = lev[k + 1, first : first + LINES, :]
            dz = lev[k + 2, first : first + LINES, :] - lev[k, first : first + LINES, :]
            dx = lev[k + 1, first + 1 : first + LINES + 1, :] - lev[k + 1, first - 1 : first + LINES - 1, :]
            right = jnp.where(lane == WIDTH - 1, 0.0, pltpu.roll(here, WIDTH - 1, 1))
            left = jnp.where(lane == 0, 0.0, pltpu.roll(here, 1, 1))
            dy = right - left
            slope = jnp.sqrt(dz * dz + dx * dx + dy * dy + 1.0)
            kap[k, block * LINES : (block + 1) * LINES, :] = (0.5 * time_step) * jnp.abs(here) * slope

    @pl.loop(1, DEPTH - 1)
    def _(k):
        growth(k)

    for copy in tiles:
        copy.wait_recv()

    shape = (3 * LINES, WIDTH)
    row_at = (block_id - 1) * LINES + lax.broadcasted_iota(jnp.int32, shape, 0)
    column_at = lax.broadcasted_iota(jnp.int32, shape, 1)
    within = jnp.logical_and(row_at >= 0, row_at <= TOP_ROW)
    has_up = row_at != 0
    has_down = row_at != TOP_ROW
    has_left = column_at != 0
    has_right = column_at != WIDTH - 1

    def from_up(v):
        return pltpu.roll(v, 1, 0)

    def from_down(v):
        return pltpu.roll(v, 3 * LINES - 1, 0)

    def from_left(v):
        return pltpu.roll(v, 1, 1)

    def from_right(v):
        return pltpu.roll(v, WIDTH - 1, 1)

    sides = ((from_down, has_down), (from_up, has_up), (from_right, has_right), (from_left, has_left))
    conduct = jnp.where(within, around[0], 0.0)
    residue = jnp.where(within, around[1], 0.0)
    diagonal = jnp.full(shape, leak_rate, F32)
    weights = []
    for shift, inside in sides:
        face = 0.5 * (conduct + jnp.where(inside, shift(conduct), 0.0))
        diagonal = diagonal + face
        weights.append(jnp.where(inside, face, 0.0))
    inverse = 1.0 / diagonal
    center = (cheb_high + cheb_low) / 2
    radius = (cheb_high - cheb_low) / 2
    sigma_ratio = center / radius
    rho_prev = 1.0 / sigma_ratio
    pressure = jnp.zeros(shape, F32)
    direction = residue * inverse * (1.0 / center)
    for sweep_index in range(ITERS):
        pressure = pressure + direction
        if sweep_index < ITERS - 1:
            image = diagonal * direction
            for weight, (shift, _) in zip(weights, sides):
                image = image - weight * shift(direction)
            residue = residue - image
            rho_next = 1.0 / (2 * sigma_ratio - rho_prev)
            direction = rho_next * rho_prev * direction + (2 * rho_next / radius) * (residue * inverse)
            rho_prev = rho_next
    grad = []
    for shift, inside in sides:
        grad.append(jnp.where(inside, shift(pressure), 0.0))
    grad_x = 0.5 * (grad[0] - grad[1])
    grad_y = 0.5 * (grad[2] - grad[3])
    flux = (conduct * (grad_x * grad_x + grad_y * grad_y) + 0.05)[LINES : 2 * LINES]
    total = flux[:, 0:STRIP]
    for c in range(1, WIDTH // STRIP):
        total = total + flux[:, c * STRIP : (c + 1) * STRIP]
    sums[0] = jnp.sum(total, axis=0, keepdims=True)

    def sum_blocks(k):
        return send(sums.at[0], sums.at[k], as_sem.at[k], ar_sem.at[k], on_across(ring(a, 2 * k)))

    def sum_plane(k):
        return send(sums_plane.at[0], sums_plane.at[k], ps_sem.at[k], pr_sem.at[k], on_plane(ring(p, k)))

    def flux_out(k):
        return send(fluxes.at[z], fluxes.at[z], fs_sem.at[k], fr_sem.at[k], on_across(ring(a, 2 * k)))

    def press_out(k):
        return send(
            press.at[lax.rem(z + k, BLOCKS)], press_got.at[z], ts_sem.at[k], tr_sem.at[k],
            on_across(ring(a, 2 * k)),
        )

    @pl.loop(0, LAST)
    def _(c):
        sum_blocks(far_first(c)).start()

    fluxes[z] = flux

    @pl.loop(0, BLOCKS)
    def _(reached):
        @pl.when(reached != z)
        def _():
            flux_out(lax.rem(reached - z + BLOCKS, BLOCKS)).start()

    @pl.when(partner_has_both)
    def _():
        layer_hop.wait_recv()
        layer_turn.start()


    for c in range(BLOCKS):
        press[c] = pressure[LINES : 2 * LINES, c * STRIP : (c + 1) * STRIP]
    press_got[z] = press[z]

    @pl.loop(1, BLOCKS)
    def _(k):
        sum_blocks(k).wait_recv()

    total = sums[0]
    for k in range(1, BLOCKS):
        total = total + sums[k]
    sums_plane[0] = total

    @pl.loop(1, GROUP)
    def _(k):
        sum_plane(k).start()

    @pl.loop(1, BLOCKS)
    def _(k):
        press_out(k).start()

    layer_same.wait_recv()

    @pl.when(has_both)
    def _():
        layer_turn.wait_recv()


    @pl.when(a == GROUP - 1)
    def _():
        lev[DEPTH + 1, PAD : PAD + ROWS, :] = jnp.zeros((ROWS, WIDTH), F32)

    growth(DEPTH - 1)

    @pl.when(a == 0)
    def _():
        lev[0, PAD : PAD + ROWS, :] = jnp.zeros((ROWS, WIDTH), F32)

    growth(0)

    @pl.loop(1, GROUP)
    def _(k):
        sum_plane(k).wait_recv()

    total = sums_plane[0]
    for k in range(1, GROUP):
        total = total + sums_plane[k]
    total = jnp.sum(total, axis=1, keepdims=True)
    scale[...] = jnp.broadcast_to(CELLS / total, scale.shape)

    @pl.loop(1, BLOCKS)
    def _(k):
        flux_out(k).wait_recv()
        press_out(k).wait_recv()

    @pl.loop(0, len(VIA))
    def _(k):
        to_partner(pick(VIA, k)).wait_send()

    to_partner(LAST).wait_send()

    @pl.loop(0, LAST)
    def _(c):
        to_owner(c, mine.at[c]).wait_send()

    for c in STRAIGHT:
        to_other_owner(c).wait_send()

    for copy in [*rims, layer_same, *tiles]:
        copy.wait_send()

    @pl.when(has_both)
    def _():
        layer_hop.wait_send()

    @pl.when(partner_has_both)
    def _():
        layer_turn.wait_send()

    @pl.loop(1, BLOCKS)
    def _(k):
        sum_blocks(k).wait_send()
        flux_out(k).wait_send()
        press_out(k).wait_send()

    @pl.loop(1, GROUP)
    def _(k):
        sum_plane(k).wait_send()


def finish(lev, kap, fluxes, scale, press_got, level_new, pressure, level_at, press_at, level_sem, press_sem):
    xh = lax.rem(lax.axis_index("across"), 2)

    def store(block):
        rows = aligned(block, LINES)
        return pltpu.make_async_copy(level_at.at[:, rows, :], level_new.at[:, rows, :], level_sem.at[block])

    @pl.loop(0, BLOCKS)
    def _(block):
        rows = aligned(block, LINES)
        rows_lev = pl.ds(pl.multiple_of(block * LINES + PAD, LINES), LINES)
        norm = fluxes[block] * scale[0:1, 0:1]
        for k in range(DEPTH):
            level_at[k, rows, :] = lev[k + 1, rows_lev, :] + kap[k, rows, :] * norm
        store(block).start()

    for block in range(BLOCKS):
        piece = press_got[block]
        piece = jnp.where(xh == 1, pltpu.roll(piece, STRIP // 2, 1), piece)
        press_at[block * LINES : (block + 1) * LINES, :] = piece[:, : STRIP // 2]
    store_press = pltpu.make_async_copy(press_at, pressure, press_sem)
    store_press.start()

    @pl.loop(0, BLOCKS)
    def _(block):
        store(block).wait()

    store_press.wait()


def on_device(labels, kappa, inflow):
    vmem = functools.partial(pltpu.VMEM, dtype=F32)
    dma = lambda n: pltpu.SemaphoreType.DMA((n,))
    hbm = pl.BlockSpec(memory_space=pltpu.HBM)
    whole = pl.BlockSpec(memory_space=pltpu.VMEM)
    labels, kappa, inflow = (pltpu.with_memory_space_constraint(x, pltpu.HBM) for x in (labels, kappa, inflow))
    parts = pl.pallas_call(
        kernel,
        out_shape=(
            jax.ShapeDtypeStruct((DEPTH + 2, ROWS + 2 * PAD, WIDTH), F32),
            jax.ShapeDtypeStruct((DEPTH, ROWS, WIDTH), F32),
            jax.ShapeDtypeStruct((BLOCKS, LINES, WIDTH), F32),
            jax.ShapeDtypeStruct((LINES, STRIP), F32),
            jax.ShapeDtypeStruct((BLOCKS, LINES, STRIP), F32),
        ),
        in_specs=[hbm, hbm, hbm],
        out_specs=(whole,) * 5,
        scratch_shapes=[
            pltpu.VMEM((DEPTH, ROWS, WIDTH), jnp.int32),
            vmem((LINES, HALF)),
            vmem((2, BLOCKS, 2, LINES, HALF)),
            vmem((BLOCKS, 2, LINES, HALF)),
            vmem((LAST, 2, LINES, HALF)),
            vmem((LAST, 2, LINES, HALF)),
            vmem((LAST, 2, LINES, HALF)),
            vmem((ROWS, WIDTH)),
            vmem((2, DEPTH, WIDTH)),
            vmem((2, DEPTH, WIDTH)),
            vmem((2, LINES, HALF)),
            vmem((2, 3 * LINES, WIDTH)),
            vmem((BLOCKS, 1, STRIP)),
            vmem((GROUP, 1, STRIP)),
            vmem((BLOCKS, LINES, STRIP)),
            dma(BLOCKS), dma(BLOCKS), pltpu.SemaphoreType.DMA,
            dma(BLOCKS), dma(BLOCKS),
            dma(BLOCKS), dma(BLOCKS), dma(BLOCKS), dma(BLOCKS),
            dma(5), dma(5),
            dma(BLOCKS), dma(BLOCKS), dma(GROUP), dma(GROUP),
            dma(BLOCKS), dma(BLOCKS), dma(BLOCKS), dma(BLOCKS),
            dma(3), dma(3), dma(2), dma(2),
        ],
        compiler_params=pltpu.CompilerParams(
            collective_id=0, has_side_effects=True, vmem_limit_bytes=32 * 2**20
        ),
        cost_estimate=pl.CostEstimate(
            flops=60 * DEPTH * ROWS * WIDTH, bytes_accessed=8 * DEPTH * ROWS * WIDTH,
            transcendentals=2 * DEPTH * ROWS * WIDTH,
        ),
        name="step",
    )(labels, kappa, inflow)
    return pl.pallas_call(
        finish,
        out_shape=(
            jax.ShapeDtypeStruct((DEPTH, ROWS, WIDTH), F32),
            jax.ShapeDtypeStruct((ROWS, STRIP // 2), F32),
        ),
        in_specs=[whole] * 5,
        out_specs=(hbm, hbm),
        scratch_shapes=[
            vmem((DEPTH, ROWS, WIDTH)),
            vmem((ROWS, STRIP // 2)),
            dma(BLOCKS),
            pltpu.SemaphoreType.DMA,
        ],
        compiler_params=pltpu.CompilerParams(vmem_limit_bytes=16 * 2**20),
        cost_estimate=pl.CostEstimate(
            flops=2 * DEPTH * ROWS * WIDTH, bytes_accessed=4 * DEPTH * ROWS * WIDTH, transcendentals=0
        ),
        name="finish",
    )(*parts)


def solution(mesh):
    return jax.shard_map(
        on_device,
        mesh=mesh,
        in_specs=(P("across", "plane", None), P("across", "plane", None), P("plane", None)),
        out_specs=(P("across", "plane", None), P("plane", "across")),
        check_vma=False,
    )
```
